32 devices in a mesh: ens: 4 (over z), polar: 2 (over core), azimuth: 4 (over y, x).
Axes of the slice: x: 2, y: 2, z: 4, core: 2. Of those that a mesh axis runs over, the one named last changes fastest.
Arguments:
- fields: bfloat16 [4, 16, 1440, 256], P('ens', 'polar', 'azimuth'), may hold values from -6 to 6
- basis_spectra: bfloat16 [9, 8, 5, 720], P(None, 'polar'), may hold values from -3 to 3
- support: int32 [8, 2], P('polar'), may hold values from 0 to 4, as said below
- weights: bfloat16 [9, 256, 256], replicated, may hold values from -0.125 to 0.125
- out_grad: bfloat16 [4, 8, 720, 256], P('ens', 'polar', 'azimuth'), may hold values from -6 to 6
Outputs:
- conv_out: bfloat16 [4, 8, 720, 256], P('ens', 'polar', 'azimuth')
- field_grad: bfloat16 [4, 16, 1440, 256], P('ens', 'polar', 'azimuth')
- weight_grad: float32 [9, 256, 256], P(None, 'azimuth')
The draws below stay inside these ranges and needn't reach their ends.
Inputs may be any that keep to these rules, and one draw needn't show every extreme that they name: Row o uses window rows support[o, 0] to support[o, 1]; support[o, 0] <= 2 <= support[o, 1]; rows o with o mod 4 equal to 0 or 3 use the whole window.
All inputs are finite; a program needn't handle non-finite values.
Results may differ from the reference program's by a relative error of at most 0.02.
Values may be sent and summed in bfloat16 or wider, within the bound.
A program may use at most 64 MiB of HBM per device.

```python
import math
import jax
import jax.numpy as jnp
from jax import lax

C = 256
K = 9
WIN = 1440
SUPPORT = 5
WOUT = 720
MODES = 360
HOUT = 8
HIN = 16
MEMBERS = 4


def draw_support(key, part):
    rows_all = jnp.arange(HOUT, dtype=jnp.int32)
    centre = SUPPORT // 2
    low_rows = jax.random.randint(jax.random.fold_in(key, 11), (HOUT,), 0, centre + 1)
    high_rows = jax.random.randint(jax.random.fold_in(key, 12), (HOUT,), centre, SUPPORT)
    whole_rows = (rows_all % 4 == 0) | (rows_all % 4 == 3)
    low_rows = jnp.where(whole_rows, 0, low_rows)
    high_rows = jnp.where(whole_rows, SUPPORT - 1, high_rows)
    return jnp.stack([low_rows, high_rows], axis=1).astype(jnp.int32)


def level_of(key, shape, shards, smallest, top_value):
    def one(axis_at, blocks):
        draws = jax.random.uniform(jax.random.fold_in(jax.random.fold_in(key, 6), axis_at), (blocks,), jnp.float32, smallest / len(shards), top_value / len(shards))
        return jnp.repeat(jnp.exp(draws), shape[axis_at] // blocks).reshape((-1,) + (1,) * (len(shape) - axis_at - 1))

    loudness = one(*shards[0])
    for cut in shards[1:]:
        loudness = loudness * one(*cut)
    return loudness


def normal_values(stream_key, dims, spread, most, cuts=(), held_as=jnp.bfloat16):
    array = jax.random.normal(stream_key, dims, jnp.float32) * spread
    if len(cuts) > 0:
        array = level_of(stream_key, dims, cuts, -0.22, 0.18) * array
    return jnp.clip(array, min=-most, max=most).astype(held_as)


def setup_inputs(seed: int = 0) -> dict:
    keys = jax.random.split(jax.random.key(seed), 6)
    return {
        "fields": normal_values(keys[0], (MEMBERS, HIN, WIN, C), 1.0, 6.0, ((0, 4), (1, 2), (2, 4))),
        "basis_spectra": normal_values(keys[1], (K, HOUT, SUPPORT, WOUT), 0.45, 3.0, ((1, 2),)),
        "support": draw_support(jax.random.fold_in(keys[5], 71), 0),
        "weights": normal_values(keys[3], (K, C, C), (K * C) ** -0.5, 0.125),
        "out_grad": normal_values(keys[4], (MEMBERS, HOUT, WOUT, C), 1.0, 6.0, ((0, 4), (1, 2), (2, 4))),
    }


def make_tables(width_in, width_out):
    mode_count = width_out // 2
    longitude = jnp.arange(width_in, dtype=jnp.int32)
    frequency = jnp.arange(mode_count, dtype=jnp.int32)
    phases = (longitude[:, None] * frequency[None, :]) % width_in
    angles = phases.astype(jnp.float32) * (2.0 * math.pi / width_in)
    forward = jnp.concatenate([jnp.cos(angles), -jnp.sin(angles)], axis=1).astype(jnp.bfloat16)
    targets = jnp.arange(width_out, dtype=jnp.int32)
    phases_out = (frequency[:, None] * targets[None, :]) % width_out
    angles_out = phases_out.astype(jnp.float32) * (2.0 * math.pi / width_out)
    factors = jnp.where(frequency == 0, 1.0, 2.0).astype(jnp.float32)[:, None] / width_in
    inverse = jnp.concatenate([factors * jnp.cos(angles_out), -factors * jnp.sin(angles_out)], axis=0).astype(jnp.bfloat16)
    return forward, inverse


def mask_filters(filters, support):
    window = jnp.arange(filters.shape[2], dtype=jnp.int32)
    inside = (window[None, :] >= support[:, 0:1]) & (window[None, :] <= support[:, 1:2])
    return jnp.where(inside[None, :, :, None], filters, jnp.zeros_like(filters))


def combine_rows(masked, spectra, mode_count):
    outputs = masked.shape[1]
    total_re = jnp.zeros((masked.shape[0], outputs, spectra.shape[1], mode_count), jnp.float32)
    total_im = jnp.zeros_like(total_re)
    for offset in range(masked.shape[2]):
        rows_at = spectra[offset: offset + 2 * outputs - 1: 2]
        real_in = rows_at[None, :, :, :mode_count]
        imag_in = rows_at[None, :, :, mode_count:]
        filter_now = masked[:, :, offset, None, :].astype(jnp.float32)
        filter_re = filter_now[..., :mode_count]
        filter_im = filter_now[..., mode_count:]
        total_re = total_re + filter_re * real_in - filter_im * imag_in
        total_im = total_im + filter_re * imag_in + filter_im * real_in
    return jnp.concatenate([total_re, total_im], axis=-1)


def spread_rows(masked, grads, mode_count, rows_total):
    outputs = masked.shape[1]
    result = jnp.zeros((rows_total, grads.shape[2], grads.shape[3]), jnp.float32)
    grad_re = grads[..., :mode_count]
    grad_im = grads[..., mode_count:]
    for offset in range(masked.shape[2]):
        filter_now = masked[:, :, offset, None, :].astype(jnp.float32)
        filter_re = filter_now[..., :mode_count]
        filter_im = filter_now[..., mode_count:]
        back_re = jnp.sum(filter_re * grad_re + filter_im * grad_im, axis=0)
        back_im = jnp.sum(filter_re * grad_im - filter_im * grad_re, axis=0)
        result = result.at[offset: offset + 2 * outputs - 1: 2].add(jnp.concatenate([back_re, back_im], axis=-1))
    return result


def reference(fields, basis_spectra, support, weights, out_grad):
    forward, inverse = make_tables(WIN, WOUT)
    masked = mask_filters(basis_spectra, support)
    margin = SUPPORT // 2
    weights_wide = weights.astype(jnp.float32)
    inverse_wide = inverse.astype(jnp.float32)

    def member_pass(pair):
        field_one = jnp.swapaxes(pair[0], 1, 2)
        cotangent = pair[1]
        padded = jnp.pad(field_one, ((margin, margin), (0, 0), (0, 0)))
        rows_total = padded.shape[0]
        spectra = jnp.dot(padded.reshape(-1, WIN), forward, preferred_element_type=jnp.float32).reshape(rows_total, C, WOUT)
        mixed_spec = combine_rows(masked, spectra, MODES).astype(jnp.bfloat16)
        mixed_wide = mixed_spec.astype(jnp.float32)
        out_spec = jnp.einsum("khcm,kcd->hdm", mixed_wide, weights_wide).astype(jnp.bfloat16)
        conv_one = jnp.dot(out_spec.reshape(-1, WOUT), inverse, preferred_element_type=jnp.float32)
        conv_one = conv_one.reshape(HOUT, C, WOUT).astype(jnp.bfloat16)
        grad_spec = jnp.einsum("hvd,mv->hdm", cotangent.astype(jnp.float32), inverse_wide).astype(jnp.bfloat16)
        grad_wide = grad_spec.astype(jnp.float32)
        weight_part = jnp.einsum("khcm,hdm->kcd", mixed_wide, grad_wide)
        mixed_grad = jnp.einsum("kcd,hdm->khcm", weights_wide, grad_wide)
        spectra_grad = spread_rows(masked, mixed_grad, MODES, rows_total)[margin: margin + HIN].astype(jnp.bfloat16)
        field_one_grad = jnp.dot(spectra_grad.reshape(-1, WOUT), forward.T, preferred_element_type=jnp.float32)
        field_one_grad = field_one_grad.reshape(HIN, C, WIN).astype(jnp.bfloat16)
        return jnp.swapaxes(conv_one, 1, 2), jnp.swapaxes(field_one_grad, 1, 2), weight_part

    conv_out, field_grad, weight_parts = lax.map(member_pass, (fields, out_grad))
    weight_grad = jnp.sum(weight_parts, axis=0)
    return conv_out, field_grad, weight_grad
```

```python
import math

import jax
import jax.numpy as jnp
import ml_dtypes
import numpy as np
from jax import lax
from jax.experimental import pallas as pl
from jax.experimental.pallas import tpu as pltpu
from jax.sharding import PartitionSpec as P

LANES = 128
ROWS = 16
F32 = jnp.float32
BF16 = jnp.bfloat16
NT = (((1,), (1,)), ((), ()))


def padded_modes(modes):
    return -(-modes // LANES) * LANES


def make_tables(width_in, width_out, shares):
    modes = width_out // 2
    wide = padded_modes(modes)
    frequency = np.arange(modes)
    phases = np.arange(width_in)[:, None] * frequency[None, :] % width_in
    angles = (phases.astype(np.float32) * np.float32(2.0 * math.pi / width_in)).astype(np.float64)
    forward = np.zeros((width_in, 2, wide), np.float32)
    forward[:, 0, :modes] = np.cos(angles)
    forward[:, 1, :modes] = -np.sin(angles)
    phases = frequency[:, None] * np.arange(width_out)[None, :] % width_out
    angles = (phases.astype(np.float32) * np.float32(2.0 * math.pi / width_out)).astype(np.float64)
    factors = (np.where(frequency == 0, 1.0, 2.0) / width_in)[:, None]
    inverse = np.zeros((2, wide, width_out), np.float32)
    inverse[0, :modes] = factors * np.cos(angles)
    inverse[1, :modes] = -factors * np.sin(angles)
    forward = forward.reshape(shares, width_in // shares, 2 * wide).astype(ml_dtypes.bfloat16)
    inverse = inverse.reshape(2 * wide, shares, width_out // shares).astype(ml_dtypes.bfloat16)
    return (
        forward,
        np.ascontiguousarray(forward.transpose(0, 2, 1)),
        np.ascontiguousarray(inverse.transpose(1, 0, 2)),
        np.ascontiguousarray(inverse.transpose(1, 2, 0)),
    )


def filter_rows(basis, support):
    k, outs, window, columns = basis.shape
    modes = columns // 2
    at = jnp.arange(window, dtype=jnp.int32)
    inside = (at[None, :] >= support[:, 0:1]) & (at[None, :] <= support[:, 1:2])
    masked = jnp.where(inside[None, :, :, None], basis, jnp.zeros_like(basis)).astype(F32)
    masked = masked.reshape(k, outs, 2 * window, modes).transpose(1, 0, 2, 3)
    extra = -(2 * window) % 8
    return jnp.pad(masked, ((0, 0), (0, 0), (0, extra), (0, padded_modes(modes) - modes)))


def whole(shape):
    return pl.BlockSpec(shape, lambda i: (0,) * len(shape))


def params():
    return pltpu.CompilerParams(
        dimension_semantics=("arbitrary",), vmem_limit_bytes=40 * 1024 * 1024
    )


def cost(flops, moved):
    return pl.CostEstimate(flops=int(flops), bytes_accessed=int(moved), transcendentals=0)


def back_kernel(window, og_ref, inv_ref, w_ref, mk_ref, gs_ref, sg_ref, mg_ref):
    o = pl.program_id(0)
    shares = og_ref.shape[0]
    taps, share, columns = mg_ref.shape
    wide = columns // 2
    block = min(ROWS, share)

    @pl.when(o == 0)
    def _():
        sg_ref[...] = jnp.zeros_like(sg_ref)

    total = jnp.dot(inv_ref[0], og_ref[0, 0], preferred_element_type=F32)
    for s in range(1, shares):
        total += jnp.dot(inv_ref[s], og_ref[s, 0], preferred_element_type=F32)
    gs = total.astype(BF16)
    gs_ref[0] = gs
    for k in range(taps):
        mg_ref[k] = lax.dot_general(w_ref[k], gs, NT, preferred_element_type=F32)

    for at in range(0, wide, LANES):
        re = slice(at, at + LANES)
        im = slice(wide + at, wide + at + LANES)

        @pl.loop(0, share // block)
        def _(c):
            rows = pl.ds(pl.multiple_of(c * block, block), block)
            acc = [[None, None] for _ in range(window)]
            for k in range(taps):
                gr = mg_ref[k, rows, re]
                gi = mg_ref[k, rows, im]
                for j in range(window):
                    pr = mk_ref[0, k, 2 * j : 2 * j + 1, re]
                    pi = mk_ref[0, k, 2 * j + 1 : 2 * j + 2, re]
                    br = pr * gr + pi * gi
                    bi = pr * gi - pi * gr
                    acc[j][0] = br if k == 0 else acc[j][0] + br
                    acc[j][1] = bi if k == 0 else acc[j][1] + bi
            for j in range(window):
                sg_ref[2 * o + j, rows, re] += acc[j][0]
                sg_ref[2 * o + j, rows, im] += acc[j][1]


def backward_spectra(gathered, inverse, weights, filters, window, rows_total):
    shares, outs, part, d = gathered.shape
    taps, share, _ = weights.shape
    columns = inverse.shape[1]
    return pl.pallas_call(
        lambda *refs: back_kernel(window, *refs),
        grid=(outs,),
        in_specs=[
            pl.BlockSpec((shares, 1, part, d), lambda i: (0, i, 0, 0)),
            whole(inverse.shape),
            whole(weights.shape),
            pl.BlockSpec((1,) + filters.shape[1:], lambda i: (i, 0, 0, 0)),
        ],
        out_specs=[
            pl.BlockSpec((1, columns, d), lambda i: (i, 0, 0)),
            whole((rows_total, share, columns)),
        ],
        out_shape=[
            jax.ShapeDtypeStruct((outs, columns, d), BF16),
            jax.ShapeDtypeStruct((rows_total, share, columns), F32),
        ],
        scratch_shapes=[pltpu.VMEM((taps, share, columns), F32)],
        compiler_params=params(),
        cost_estimate=cost(2e10, 1e7),
    )(gathered, inverse, weights, filters)


def field_grad_kernel(sg_ref, low_ref, high_ref, table_ref, out_ref):
    i = pl.program_id(0)
    last = pl.num_programs(0) - 1
    rows, share, columns = sg_ref.shape
    low = jnp.where(i == 0, low_ref[...].astype(F32), 0.0)
    high = jnp.where(i == last, high_ref[...].astype(F32), 0.0)
    value = (sg_ref[...] + low + high).astype(BF16).reshape(rows * share, columns)
    for s in range(table_ref.shape[0]):
        piece = jnp.dot(value, table_ref[s], preferred_element_type=F32)
        out_ref[s] = piece.astype(BF16).reshape(rows, share, piece.shape[1])


def field_gradient(sg, low, high, table):
    rim, share, columns = low.shape
    rows = sg.shape[0] - 2 * rim
    shares, _, part = table.shape
    return pl.pallas_call(
        field_grad_kernel,
        grid=(rows // rim,),
        in_specs=[
            pl.BlockSpec((rim, share, columns), lambda i: (i + 1, 0, 0)),
            whole(low.shape),
            whole(high.shape),
            whole(table.shape),
        ],
        out_specs=pl.BlockSpec((shares, rim, share, part), lambda i: (0, i, 0, 0)),
        out_shape=jax.ShapeDtypeStruct((shares, rows, share, part), BF16),
        compiler_params=params(),
        cost_estimate=cost(5e9, 6e6),
    )(sg, low, high, table)


def spectra_kernel(x_ref, table_ref, out_ref):
    shares, rows, share, part = x_ref.shape
    total = None
    for s in range(shares):
        term = jnp.dot(
            x_ref[s].reshape(rows * share, part), table_ref[s], preferred_element_type=F32
        )
        total = term if total is None else total + term
    out_ref[...] = total.reshape(out_ref.shape)


def input_spectra(x, table, rim):
    shares, rows, share, part = x.shape
    columns = table.shape[2]
    return pl.pallas_call(
        spectra_kernel,
        grid=(rows // rim,),
        in_specs=[
            pl.BlockSpec((shares, rim, share, part), lambda i: (0, i, 0, 0)),
            whole(table.shape),
        ],
        out_specs=pl.BlockSpec((rim, share, columns), lambda i: (i, 0, 0)),
        out_shape=jax.ShapeDtypeStruct((rows, share, columns), F32),
        compiler_params=params(),
        cost_estimate=cost(5e9, 6e6),
    )(x, table)


def mix_kernel(window, x_ref, low_ref, high_ref, mk_ref, gs_ref, wt_ref, inv_ref,
               conv_ref, wg_ref, ext_ref, mixed_ref, total_ref):
    o = pl.program_id(0)
    rows, share, columns = x_ref.shape
    rim = low_ref.shape[0]
    taps = mixed_ref.shape[0]
    wide = columns // 2
    block = min(ROWS, share)

    @pl.when(o == 0)
    def _():
        ext_ref[0:rim] = low_ref[...].astype(F32)
        ext_ref[rim : rim + rows] = x_ref[...]
        ext_ref[rim + rows :] = high_ref[...].astype(F32)
        total_ref[...] = jnp.zeros_like(total_ref)

    for at in range(0, wide, LANES):
        re = slice(at, at + LANES)
        im = slice(wide + at, wide + at + LANES)

        @pl.loop(0, share // block)
        def _(c):
            here = pl.ds(pl.multiple_of(c * block, block), block)
            xr = [ext_ref[2 * o + j, here, re] for j in range(window)]
            xi = [ext_ref[2 * o + j, here, im] for j in range(window)]
            for k in range(taps):
                mr = mi = None
                for j in range(window):
                    pr = mk_ref[0, k, 2 * j : 2 * j + 1, re]
                    pi = mk_ref[0, k, 2 * j + 1 : 2 * j + 2, re]
                    tr = pr * xr[j] - pi * xi[j]
                    ti = pr * xi[j] + pi * xr[j]
                    mr = tr if j == 0 else mr + tr
                    mi = ti if j == 0 else mi + ti
                mixed_ref[k, here, re] = mr.astype(BF16)
                mixed_ref[k, here, im] = mi.astype(BF16)

    mixed = mixed_ref[...].reshape(taps * share, columns)
    total_ref[...] += jnp.dot(mixed, gs_ref[0], preferred_element_type=F32)
    spec = jnp.dot(wt_ref[...], mixed, preferred_element_type=F32).astype(BF16)
    for s in range(inv_ref.shape[0]):
        conv_ref[s, 0] = lax.dot_general(
            inv_ref[s], spec, NT, preferred_element_type=F32
        ).astype(BF16)

    @pl.when(o == pl.num_programs(0) - 1)
    def _():
        wg_ref[...] = total_ref[...].astype(BF16)


def mix(x, low, high, filters, gs, weights_t, inverse_t, window):
    rows, share, columns = x.shape
    rim = low.shape[0]
    outs, taps = filters.shape[:2]
    d = gs.shape[2]
    shares, part, _ = inverse_t.shape
    return pl.pallas_call(
        lambda *refs: mix_kernel(window, *refs),
        grid=(outs,),
        in_specs=[
            whole(x.shape),
            whole(low.shape),
            whole(high.shape),
            pl.BlockSpec((1,) + filters.shape[1:], lambda i: (i, 0, 0, 0)),
            pl.BlockSpec((1, columns, d), lambda i: (i, 0, 0)),
            whole(weights_t.shape),
            whole(inverse_t.shape),
        ],
        out_specs=[
            pl.BlockSpec((shares, 1, part, d), lambda i: (0, i, 0, 0)),
            whole((taps * share, d)),
        ],
        out_shape=[
            jax.ShapeDtypeStruct((shares, outs, part, d), BF16),
            jax.ShapeDtypeStruct((taps * share, d), BF16),
        ],
        scratch_shapes=[
            pltpu.VMEM((rows + 2 * rim, share, columns), F32),
            pltpu.VMEM((taps, share, columns), BF16),
            pltpu.VMEM((taps * share, d), F32),
        ],
        compiler_params=params(),
        cost_estimate=cost(2e10, 1e7),
    )(x, low, high, filters, gs, weights_t, inverse_t)


def to_neighbours(first, last):
    count = lax.axis_size("polar")
    up = [(i, i + 1) for i in range(count - 1)]
    down = [(i + 1, i) for i in range(count - 1)]
    return lax.ppermute(last, "polar", up), lax.ppermute(first, "polar", down)


def local(fields, basis_spectra, support, weights, out_grad):
    shares = lax.axis_size("azimuth")
    window = basis_spectra.shape[2]
    margin = window // 2
    _, rows, part, channels = fields.shape
    share = channels // shares
    taps, _, d = weights.shape
    forward, forward_t, inverse, inverse_t = make_tables(
        part * shares, out_grad.shape[2] * shares, shares
    )
    gathered = lax.all_gather(out_grad[0], "azimuth", axis=0)
    pieces = fields[0].reshape(rows, part, shares, share).transpose(2, 0, 3, 1)
    spread = lax.all_to_all(pieces, "azimuth", 0, 0)
    filters = filter_rows(basis_spectra, support)
    own = lax.dynamic_slice_in_dim(weights, lax.axis_index("azimuth") * share, share, 1)
    own_t = own.reshape(taps * share, d).T

    gs, sg = backward_spectra(
        gathered, jnp.asarray(inverse), own, filters, window, rows + 2 * margin
    )
    low, high = to_neighbours(sg[:margin].astype(BF16), sg[margin + rows :].astype(BF16))
    grad_pieces = field_gradient(sg, low, high, jnp.asarray(forward_t))
    grad_back = lax.all_to_all(grad_pieces, "azimuth", 0, 0)

    x = input_spectra(spread, jnp.asarray(forward), margin)
    low, high = to_neighbours(x[:margin].astype(BF16), x[rows - margin :].astype(BF16))
    conv_parts, wg = mix(x, low, high, filters, gs, own_t, jnp.asarray(inverse_t), window)

    axes = ("ens", "polar")
    count = lax.axis_size("ens") * lax.axis_size("polar")
    terms = lax.all_to_all(wg.reshape(count, -1, d), axes, 0, 0)
    conv_terms = lax.all_to_all(conv_parts, "azimuth", 0, 0)
    summed = jnp.sum(terms.astype(F32), axis=0).astype(BF16)
    weight_grad = lax.all_gather(summed, axes, axis=0, tiled=True)
    weight_grad = weight_grad.reshape(taps, share, d).astype(F32)
    conv_out = jnp.sum(conv_terms.astype(F32), axis=0).astype(BF16)
    field_grad = grad_back.transpose(1, 3, 0, 2).reshape(rows, part, channels)
    return (conv_out[None], field_grad[None], weight_grad)


def solution(mesh):
    placed = (
        P("ens", "polar", "azimuth", None),
        P(None, "polar", None, None),
        P("polar", None),
        P(),
        P("ens", "polar", "azimuth", None),
    )
    return jax.shard_map(
        local,
        mesh=mesh,
        in_specs=placed,
        out_specs=(
            P("ens", "polar", "azimuth", None),
            P("ens", "polar", "azimuth", None),
            P(None, "azimuth", None),
        ),
        check_vma=False,
    )
```

```python
import math

import jax
import jax.numpy as jnp
import ml_dtypes
import numpy as np
from jax import lax
from jax.experimental import pallas as pl
from jax.experimental.pallas import tpu as pltpu
from jax.sharding import PartitionSpec as P

LANES = 128
ROWS = 16
F32 = jnp.float32
BF16 = jnp.bfloat16
NT = (((1,), (1,)), ((), ()))


def padded_modes(modes):
    return -(-modes // LANES) * LANES


def make_tables(width_in, width_out, shares):
    modes = width_out // 2
    wide = padded_modes(modes)
    frequency = np.arange(modes)
    phases = np.arange(width_in)[:, None] * frequency[None, :] % width_in
    angles = (phases.astype(np.float32) * np.float32(2.0 * math.pi / width_in)).astype(np.float64)
    forward = np.zeros((width_in, 2, wide), np.float32)
    forward[:, 0, :modes] = np.cos(angles)
    forward[:, 1, :modes] = -np.sin(angles)
    phases = frequency[:, None] * np.arange(width_out)[None, :] % width_out
    angles = (phases.astype(np.float32) * np.float32(2.0 * math.pi / width_out)).astype(np.float64)
    factors = (np.where(frequency == 0, 1.0, 2.0) / width_in)[:, None]
    inverse = np.zeros((2, wide, width_out), np.float32)
    inverse[0, :modes] = factors * np.cos(angles)
    inverse[1, :modes] = -factors * np.sin(angles)
    forward = forward.reshape(shares, width_in // shares, 2 * wide).astype(ml_dtypes.bfloat16)
    inverse = inverse.reshape(2 * wide, shares, width_out // shares).astype(ml_dtypes.bfloat16)
    return (
        forward,
        np.ascontiguousarray(forward.transpose(0, 2, 1)),
        np.ascontiguousarray(inverse.transpose(1, 0, 2)),
        np.pad(inverse.transpose(1, 2, 0), ((0, 0), (0, -inverse.shape[2] % ROWS), (0, 0))),
    )


def filter_rows(basis, support):
    k, outs, window, columns = basis.shape
    modes = columns // 2
    at = jnp.arange(window, dtype=jnp.int32)
    inside = (at[None, :] >= support[:, 0:1]) & (at[None, :] <= support[:, 1:2])
    masked = jnp.where(inside[None, :, :, None], basis, jnp.zeros_like(basis)).astype(F32)
    masked = masked.reshape(k, outs, 2 * window, modes).transpose(1, 0, 2, 3)
    extra = -(2 * window) % 8
    return jnp.pad(masked, ((0, 0), (0, 0), (0, extra), (0, padded_modes(modes) - modes)))


def whole(shape):
    return pl.BlockSpec(shape, lambda i: (0,) * len(shape))


def params():
    return pltpu.CompilerParams(
        dimension_semantics=("arbitrary",), vmem_limit_bytes=40 * 1024 * 1024
    )


def cost(flops, moved):
    return pl.CostEstimate(flops=int(flops), bytes_accessed=int(moved), transcendentals=0)


def back_kernel(window, og_ref, inv_ref, w_ref, mk_ref, gs_ref, sg_ref, mg_ref):
    o = pl.program_id(0)
    shares = og_ref.shape[0]
    taps, share, columns = mg_ref.shape
    wide = columns // 2
    block = min(ROWS, share)

    @pl.when(o == 0)
    def _():
        sg_ref[...] = jnp.zeros_like(sg_ref)

    total = jnp.dot(inv_ref[0], og_ref[0, 0], preferred_element_type=F32)
    for s in range(1, shares):
        total += jnp.dot(inv_ref[s], og_ref[s, 0], preferred_element_type=F32)
    gs = total.astype(BF16)
    gs_ref[0] = gs
    for k in range(taps):
        mg_ref[k] = lax.dot_general(w_ref[k], gs, NT, preferred_element_type=F32)

    for at in range(0, wide, LANES):
        re = slice(at, at + LANES)
        im = slice(wide + at, wide + at + LANES)

        @pl.loop(0, share // block)
        def _(c):
            rows = pl.ds(pl.multiple_of(c * block, block), block)
            acc = [[None, None] for _ in range(window)]
            for k in range(taps):
                gr = mg_ref[k, rows, re]
                gi = mg_ref[k, rows, im]
                for j in range(window):
                    pr = mk_ref[0, k, 2 * j : 2 * j + 1, re]
                    pi = mk_ref[0, k, 2 * j + 1 : 2 * j + 2, re]
                    br = pr * gr + pi * gi
                    bi = pr * gi - pi * gr
                    acc[j][0] = br if k == 0 else acc[j][0] + br
                    acc[j][1] = bi if k == 0 else acc[j][1] + bi
            for j in range(window):
                sg_ref[2 * o + j, rows, re] += acc[j][0]
                sg_ref[2 * o + j, rows, im] += acc[j][1]


def backward_spectra(gathered, inverse, weights, filters, window, rows_total):
    shares, outs, part, d = gathered.shape
    taps, share, _ = weights.shape
    columns = inverse.shape[1]
    return pl.pallas_call(
        lambda *refs: back_kernel(window, *refs),
        grid=(outs,),
        in_specs=[
            pl.BlockSpec((shares, 1, part, d), lambda i: (0, i, 0, 0)),
            whole(inverse.shape),
            whole(weights.shape),
            pl.BlockSpec((1,) + filters.shape[1:], lambda i: (i, 0, 0, 0)),
        ],
        out_specs=[
            pl.BlockSpec((1, columns, d), lambda i: (i, 0, 0)),
            whole((rows_total, share, columns)),
        ],
        out_shape=[
            jax.ShapeDtypeStruct((outs, columns, d), BF16),
            jax.ShapeDtypeStruct((rows_total, share, columns), F32),
        ],
        scratch_shapes=[pltpu.VMEM((taps, share, columns), F32)],
        compiler_params=params(),
        cost_estimate=cost(2e10, 1e7),
    )(gathered, inverse, weights, filters)


def field_grad_kernel(sg_ref, low_ref, high_ref, table_ref, out_ref):
    i = pl.program_id(0)
    last = pl.num_programs(0) - 1
    rows, share, columns = sg_ref.shape
    low = jnp.where(i == 0, low_ref[...].astype(F32), 0.0)
    high = jnp.where(i == last, high_ref[...].astype(F32), 0.0)
    value = (sg_ref[...] + low + high).astype(BF16).reshape(rows * share, columns)
    for s in range(table_ref.shape[0]):
        piece = jnp.dot(value, table_ref[s], preferred_element_type=F32)
        out_ref[s] = piece.astype(BF16).reshape(rows, share, piece.shape[1])


def field_gradient(sg, low, high, table):
    rim, share, columns = low.shape
    rows = sg.shape[0] - 2 * rim
    shares, _, part = table.shape
    return pl.pallas_call(
        field_grad_kernel,
        grid=(rows // rim,),
        in_specs=[
            pl.BlockSpec((rim, share, columns), lambda i: (i + 1, 0, 0)),
            whole(low.shape),
            whole(high.shape),
            whole(table.shape),
        ],
        out_specs=pl.BlockSpec((shares, rim, share, part), lambda i: (0, i, 0, 0)),
        out_shape=jax.ShapeDtypeStruct((shares, rows, share, part), BF16),
        compiler_params=params(),
        cost_estimate=cost(5e9, 6e6),
    )(sg, low, high, table)


def spectra_kernel(x_ref, table_ref, out_ref):
    shares, rows, share, part = x_ref.shape
    total = None
    for s in range(shares):
        term = jnp.dot(
            x_ref[s].reshape(rows * share, part), table_ref[s], preferred_element_type=F32
        )
        total = term if total is None else total + term
    out_ref[...] = total.reshape(out_ref.shape)


def input_spectra(x, table, rim):
    shares, rows, share, part = x.shape
    columns = table.shape[2]
    return pl.pallas_call(
        spectra_kernel,
        grid=(rows // rim,),
        in_specs=[
            pl.BlockSpec((shares, rim, share, part), lambda i: (0, i, 0, 0)),
            whole(table.shape),
        ],
        out_specs=pl.BlockSpec((rim, share, columns), lambda i: (i, 0, 0)),
        out_shape=jax.ShapeDtypeStruct((rows, share, columns), F32),
        compiler_params=params(),
        cost_estimate=cost(5e9, 6e6),
    )(x, table)


def mix_kernel(window, x_ref, low_ref, high_ref, mk_ref, gs_ref, wt_ref, inv_ref,
               conv_ref, wg_ref, ext_ref, mixed_ref, total_ref,
               conv_send, conv_recv, piece_send, piece_recv, sums,
               conv_out_sem, conv_in_sem, piece_out_sem, piece_in_sem, sum_out_sem, sum_in_sem):
    o = pl.program_id(0)
    rows, share, columns = x_ref.shape
    rim = low_ref.shape[0]
    taps = mixed_ref.shape[0]
    wide = columns // 2
    block = min(ROWS, share)
    shares, outs = conv_send.shape[:2]
    count, piece = piece_send.shape[:2]
    part = conv_ref.shape[1]
    me = lax.axis_index("azimuth")
    bands = lax.axis_size("polar")
    rank = lax.axis_index("ens") * bands + lax.axis_index("polar")

    def across(step):
        other = lax.rem(me + step, shares)
        return other, {"azimuth": other}

    def along(step):
        other = lax.rem(rank + step, count)
        return other, {"ens": lax.div(other, bands), "polar": lax.rem(other, bands)}

    def conv_copy(row, step):
        other, device = across(step)
        return pltpu.make_async_remote_copy(
            src_ref=conv_send.at[other, row],
            dst_ref=conv_recv.at[me, row],
            send_sem=conv_out_sem.at[step, row],
            recv_sem=conv_in_sem.at[me, row],
            device_id=device,
            device_id_type=pl.DeviceIdType.MESH,
        )

    def conv_arrival(row, step):
        other, device = across(step)
        return pltpu.make_async_remote_copy(
            src_ref=conv_send.at[other, row],
            dst_ref=conv_recv.at[other, row],
            send_sem=conv_out_sem.at[step, row],
            recv_sem=conv_in_sem.at[other, row],
            device_id=device,
            device_id_type=pl.DeviceIdType.MESH,
        )

    def piece_copy(step, landing):
        other, device = along(step)
        at = rank if landing is None else other
        return pltpu.make_async_remote_copy(
            src_ref=piece_send.at[other],
            dst_ref=piece_recv.at[at],
            send_sem=piece_out_sem.at[step],
            recv_sem=piece_in_sem.at[at],
            device_id=device,
            device_id_type=pl.DeviceIdType.MESH,
        )

    def sum_copy(step, landing):
        other, device = along(step)
        at = rank if landing is None else other
        return pltpu.make_async_remote_copy(
            src_ref=sums.at[at],
            dst_ref=sums.at[at],
            send_sem=sum_out_sem.at[step],
            recv_sem=sum_in_sem.at[at],
            device_id=device,
            device_id_type=pl.DeviceIdType.MESH,
        )

    @pl.when(o == 0)
    def _():
        barrier = pltpu.get_barrier_semaphore()
        for step in range(1, shares):
            pl.semaphore_signal(
                barrier, inc=1, device_id=across(step)[1], device_id_type=pl.DeviceIdType.MESH
            )
        for step in range(1, count):
            pl.semaphore_signal(
                barrier, inc=1, device_id=along(step)[1], device_id_type=pl.DeviceIdType.MESH
            )
        pl.semaphore_wait(barrier, shares + count - 2)
        ext_ref[0:rim] = low_ref[...].astype(F32)
        ext_ref[rim : rim + rows] = x_ref[...]
        ext_ref[rim + rows :] = high_ref[...].astype(F32)
        total_ref[...] = jnp.zeros_like(total_ref)

    for at in range(0, wide, LANES):
        re = slice(at, at + LANES)
        im = slice(wide + at, wide + at + LANES)

        @pl.loop(0, share // block)
        def _(c):
            here = pl.ds(pl.multiple_of(c * block, block), block)
            xr = [ext_ref[2 * o + j, here, re] for j in range(window)]
            xi = [ext_ref[2 * o + j, here, im] for j in range(window)]
            for k in range(taps):
                mr = mi = None
                for j in range(window):
                    pr = mk_ref[0, k, 2 * j : 2 * j + 1, re]
                    pi = mk_ref[0, k, 2 * j + 1 : 2 * j + 2, re]
                    tr = pr * xr[j] - pi * xi[j]
                    ti = pr * xi[j] + pi * xr[j]
                    mr = tr if j == 0 else mr + tr
                    mi = ti if j == 0 else mi + ti
                mixed_ref[k, here, re] = mr.astype(BF16)
                mixed_ref[k, here, im] = mi.astype(BF16)

    mixed = mixed_ref[...].reshape(taps * share, columns)
    total_ref[0 : taps * share] += jnp.dot(mixed, gs_ref[0], preferred_element_type=F32)

    @pl.when(o == outs - 1)
    def _():
        for p in range(count):
            piece_send[p] = total_ref[p * piece : (p + 1) * piece].astype(BF16)
        for step in range(1, count):
            piece_copy(step, None).start()
        piece_recv[rank] = piece_send[rank]

    spec = jnp.dot(wt_ref[...], mixed, preferred_element_type=F32).astype(BF16)
    for step in list(range(1, shares)) + [0]:
        other = across(step)[0]
        term = lax.dot_general(inv_ref[other], spec, NT, preferred_element_type=F32).astype(BF16)
        if step == 0:
            conv_recv[me, o] = term
        else:
            conv_send[other, o] = term
            conv_copy(o, step).start()

    @pl.when(o == outs - 1)
    def _():
        for step in range(1, count):
            piece_copy(step, True).wait_recv()
        whole_sum = piece_recv[0].astype(F32)
        for p in range(1, count):
            whole_sum += piece_recv[p].astype(F32)
        sums[rank] = whole_sum.astype(BF16)
        for step in range(1, count):
            sum_copy(step, None).start()
        for row in range(outs):
            for step in range(1, shares):
                conv_arrival(row, step).wait_recv()
        for row in range(outs):
            result = conv_recv[0, row].astype(F32)
            for s in range(1, shares):
                result += conv_recv[s, row].astype(F32)
            conv_ref[row] = result.astype(BF16)[:part]
        for step in range(1, count):
            sum_copy(step, True).wait_recv()
        wg_ref[...] = sums[...].astype(F32).reshape(count * piece, -1)[: taps * share]
        for row in range(outs):
            for step in range(1, shares):
                conv_copy(row, step).wait_send()
        for step in range(1, count):
            piece_copy(step, None).wait_send()
            sum_copy(step, None).wait_send()


def mix(x, low, high, filters, gs, weights_t, inverse_t, window, part):
    rows, share, columns = x.shape
    rim = low.shape[0]
    outs, taps = filters.shape[:2]
    d = gs.shape[2]
    shares, padded, _ = inverse_t.shape
    count = lax.axis_size("ens") * lax.axis_size("polar")
    piece = -(-taps * share // (count * ROWS)) * ROWS
    dma = pltpu.SemaphoreType.DMA
    return pl.pallas_call(
        lambda *refs: mix_kernel(window, *refs),
        grid=(outs,),
        in_specs=[
            whole(x.shape),
            whole(low.shape),
            whole(high.shape),
            pl.BlockSpec((1,) + filters.shape[1:], lambda i: (i, 0, 0, 0)),
            pl.BlockSpec((1, columns, d), lambda i: (i, 0, 0)),
            whole(weights_t.shape),
            whole(inverse_t.shape),
        ],
        out_specs=[whole((outs, part, d)), whole((taps * share, d))],
        out_shape=[
            jax.ShapeDtypeStruct((outs, part, d), BF16),
            jax.ShapeDtypeStruct((taps * share, d), F32),
        ],
        scratch_shapes=[
            pltpu.VMEM((rows + 2 * rim, share, columns), F32),
            pltpu.VMEM((taps, share, columns), BF16),
            pltpu.VMEM((count * piece, d), F32),
            pltpu.VMEM((shares, outs, padded, d), BF16),
            pltpu.VMEM((shares, outs, padded, d), BF16),
            pltpu.VMEM((count, piece, d), BF16),
            pltpu.VMEM((count, piece, d), BF16),
            pltpu.VMEM((count, piece, d), BF16),
            dma((shares, outs)),
            dma((shares, outs)),
            dma((count,)),
            dma((count,)),
            dma((count,)),
            dma((count,)),
        ],
        compiler_params=pltpu.CompilerParams(
            dimension_semantics=("arbitrary",),
            vmem_limit_bytes=40 * 1024 * 1024,
            collective_id=0,
            has_side_effects=True,
        ),
        cost_estimate=cost(2e10, 1e7),
    )(x, low, high, filters, gs, weights_t, inverse_t)


def to_neighbours(first, last):
    count = lax.axis_size("polar")
    up = [(i, i + 1) for i in range(count - 1)]
    down = [(i + 1, i) for i in range(count - 1)]
    return lax.ppermute(last, "polar", up), lax.ppermute(first, "polar", down)


def local(fields, basis_spectra, support, weights, out_grad):
    shares = lax.axis_size("azimuth")
    window = basis_spectra.shape[2]
    margin = window // 2
    _, rows, part, channels = fields.shape
    share = channels // shares
    taps, _, d = weights.shape
    forward, forward_t, inverse, inverse_t = make_tables(
        part * shares, out_grad.shape[2] * shares, shares
    )
    gathered = lax.all_gather(out_grad[0], "azimuth", axis=0)
    pieces = fields[0].reshape(rows, part, shares, share).transpose(2, 0, 3, 1)
    spread = lax.all_to_all(pieces, "azimuth", 0, 0)
    filters = filter_rows(basis_spectra, support)
    own = lax.dynamic_slice_in_dim(weights, lax.axis_index("azimuth") * share, share, 1)
    own_t = own.reshape(taps * share, d).T

    gs, sg = backward_spectra(
        gathered, jnp.asarray(inverse), own, filters, window, rows + 2 * margin
    )
    low, high = to_neighbours(sg[:margin].astype(BF16), sg[margin + rows :].astype(BF16))
    grad_pieces = field_gradient(sg, low, high, jnp.asarray(forward_t))
    grad_back = lax.all_to_all(grad_pieces, "azimuth", 0, 0)

    spread, _ = lax.optimization_barrier((spread, grad_pieces))
    x = input_spectra(spread, jnp.asarray(forward), margin)
    low, high = to_neighbours(x[:margin].astype(BF16), x[rows - margin :].astype(BF16))
    conv_out, weight_grad = mix(
        x, low, high, filters, gs, own_t, jnp.asarray(inverse_t), window, out_grad.shape[2]
    )
    weight_grad = weight_grad.reshape(taps, share, d)
    field_grad = grad_back.transpose(1, 3, 0, 2).reshape(rows, part, channels)
    return (conv_out[None], field_grad[None], weight_grad)


def solution(mesh):
    placed = (
        P("ens", "polar", "azimuth", None),
        P(None, "polar", None, None),
        P("polar", None),
        P(),
        P("ens", "polar", "azimuth", None),
    )
    return jax.shard_map(
        local,
        mesh=mesh,
        in_specs=placed,
        out_specs=(
            P("ens", "polar", "azimuth", None),
            P("ens", "polar", "azimuth", None),
            P(None, "azimuth", None),
        ),
        check_vma=False,
    )
```

```python
import math

import jax
import jax.numpy as jnp
import ml_dtypes
import numpy as np
from jax import lax
from jax.experimental import pallas as pl
from jax.experimental.pallas import tpu as pltpu
from jax.sharding import PartitionSpec as P

LANES = 128
ROWS = 16
F32 = jnp.float32
BF16 = jnp.bfloat16
NT = (((1,), (1,)), ((), ()))


def padded_modes(modes):
    return -(-modes // LANES) * LANES


def make_tables(width_in, width_out, shares):
    modes = width_out // 2
    wide = padded_modes(modes)
    frequency = np.arange(modes)
    phases = np.arange(width_in)[:, None] * frequency[None, :] % width_in
    angles = (phases.astype(np.float32) * np.float32(2.0 * math.pi / width_in)).astype(np.float64)
    forward = np.zeros((width_in, 2, wide), np.float32)
    forward[:, 0, :modes] = np.cos(angles)
    forward[:, 1, :modes] = -np.sin(angles)
    phases = frequency[:, None] * np.arange(width_out)[None, :] % width_out
    angles = (phases.astype(np.float32) * np.float32(2.0 * math.pi / width_out)).astype(np.float64)
    factors = (np.where(frequency == 0, 1.0, 2.0) / width_in)[:, None]
    inverse = np.zeros((2, wide, width_out), np.float32)
    inverse[0, :modes] = factors * np.cos(angles)
    inverse[1, :modes] = -factors * np.sin(angles)
    forward = forward.reshape(shares, width_in // shares, 2 * wide).astype(ml_dtypes.bfloat16)
    inverse = inverse.reshape(2 * wide, shares, width_out // shares).astype(ml_dtypes.bfloat16)
    return (
        forward,
        np.ascontiguousarray(forward.transpose(0, 2, 1)),
        np.pad(inverse.transpose(1, 0, 2), ((0, 0), (0, 0), (0, -inverse.shape[2] % ROWS))),
        np.pad(inverse.transpose(1, 2, 0), ((0, 0), (0, -inverse.shape[2] % ROWS), (0, 0))),
    )


def filter_rows(basis, support):
    k, outs, window, columns = basis.shape
    modes = columns // 2
    at = jnp.arange(window, dtype=jnp.int32)
    inside = (at[None, :] >= support[:, 0:1]) & (at[None, :] <= support[:, 1:2])
    masked = jnp.where(inside[None, :, :, None], basis, jnp.zeros_like(basis)).astype(F32)
    masked = masked.reshape(k, outs, 2 * window, modes).transpose(1, 0, 2, 3)
    extra = -(2 * window) % 8
    return jnp.pad(masked, ((0, 0), (0, 0), (0, extra), (0, padded_modes(modes) - modes)))


def whole(shape):
    return pl.BlockSpec(shape, lambda i: (0,) * len(shape))


def params():
    return pltpu.CompilerParams(
        dimension_semantics=("arbitrary",), vmem_limit_bytes=40 * 1024 * 1024
    )


def remote_params(identity):
    return pltpu.CompilerParams(
        dimension_semantics=("arbitrary",),
        vmem_limit_bytes=40 * 1024 * 1024,
        collective_id=identity,
        has_side_effects=True,
    )


def cost(flops, moved):
    return pl.CostEstimate(flops=int(flops), bytes_accessed=int(moved), transcendentals=0)


def rim_copies(send, recv, out_sem, in_sem):
    bands = lax.axis_size("polar")
    band = lax.axis_index("polar")
    return [
        pltpu.make_async_remote_copy(
            src_ref=send.at[side],
            dst_ref=recv.at[1 - side],
            send_sem=out_sem.at[side],
            recv_sem=in_sem.at[1 - side],
            device_id={"polar": lax.rem(band + step, bands)},
            device_id_type=pl.DeviceIdType.MESH,
        )
        for side, step in ((0, bands - 1), (1, 1))
    ]


def rim_values(recv):
    band = lax.axis_index("polar")
    low = jnp.where(band > 0, recv[0].astype(F32), 0.0)
    high = jnp.where(band < lax.axis_size("polar") - 1, recv[1].astype(F32), 0.0)
    return low, high


def back_kernel(window, og_ref, inv_ref, w_ref, mk_ref, gs_ref, sg_ref, low_ref, high_ref,
                mg_ref, og_all, rim_send, rim_recv,
                og_out_sem, og_in_sem, rim_out_sem, rim_in_sem):
    o = pl.program_id(0)
    shares, outs = og_all.shape[:2]
    taps, share, columns = mg_ref.shape
    rim = low_ref.shape[0]
    me = lax.axis_index("azimuth")
    bands = lax.axis_size("polar")

    def og_copy(row, step, arriving):
        other = lax.rem(me + step, shares)
        at = other if arriving else me
        return pltpu.make_async_remote_copy(
            src_ref=og_ref.at[row],
            dst_ref=og_all.at[at, row],
            send_sem=og_out_sem.at[step, row],
            recv_sem=og_in_sem.at[at, row],
            device_id={"azimuth": other},
            device_id_type=pl.DeviceIdType.MESH,
        )

    @pl.when(o == 0)
    def _():
        barrier = pltpu.get_barrier_semaphore()
        for step in range(1, shares):
            pl.semaphore_signal(
                barrier,
                inc=1,
                device_id={"azimuth": lax.rem(me + step, shares)},
                device_id_type=pl.DeviceIdType.MESH,
            )
        for step in (1, bands - 1):
            pl.semaphore_signal(
                barrier,
                inc=1,
                device_id={"polar": lax.rem(lax.axis_index("polar") + step, bands)},
                device_id_type=pl.DeviceIdType.MESH,
            )
        pl.semaphore_wait(barrier, shares + 1)
        for row in range(outs):
            for step in range(1, shares):
                og_copy(row, step, False).start()

    wide = columns // 2
    block = min(ROWS, share)

    @pl.when(o == 0)
    def _():
        sg_ref[...] = jnp.zeros_like(sg_ref)

    total = jnp.dot(inv_ref[me], og_ref[o], preferred_element_type=F32)
    for step in range(1, shares):
        other = lax.rem(me + step, shares)
        og_copy(o, step, True).wait_recv()
        total += jnp.dot(inv_ref[other], og_all[other, o], preferred_element_type=F32)
    gs = total.astype(BF16)
    gs_ref[0] = gs
    for k in range(taps):
        mg_ref[k] = lax.dot_general(w_ref[k], gs, NT, preferred_element_type=F32)

    for at in range(0, wide, LANES):
        re = slice(at, at + LANES)
        im = slice(wide + at, wide + at + LANES)

        @pl.loop(0, share // block)
        def _(c):
            rows = pl.ds(pl.multiple_of(c * block, block), block)
            acc = [[None, None] for _ in range(window)]
            for k in range(taps):
                gr = mg_ref[k, rows, re]
                gi = mg_ref[k, rows, im]
                for j in range(window):
                    pr = mk_ref[0, k, 2 * j : 2 * j + 1, re]
                    pi = mk_ref[0, k, 2 * j + 1 : 2 * j + 2, re]
                    br = pr * gr + pi * gi
                    bi = pr * gi - pi * gr
                    acc[j][0] = br if k == 0 else acc[j][0] + br
                    acc[j][1] = bi if k == 0 else acc[j][1] + bi
            for j in range(window):
                sg_ref[2 * o + j, rows, re] += acc[j][0]
                sg_ref[2 * o + j, rows, im] += acc[j][1]


    @pl.when(o == outs - 1)
    def _():
        copies = rim_copies(rim_send, rim_recv, rim_out_sem, rim_in_sem)
        rim_send[0] = sg_ref[0:rim].astype(BF16)
        rim_send[1] = sg_ref[sg_ref.shape[0] - rim :].astype(BF16)
        for copy in copies:
            copy.start()
        for copy in copies:
            copy.wait_recv()
        low, high = rim_values(rim_recv)
        low_ref[...] = low.astype(BF16)
        high_ref[...] = high.astype(BF16)
        for copy in copies:
            copy.wait_send()
        for row in range(outs):
            for step in range(1, shares):
                og_copy(row, step, False).wait_send()


def backward_spectra(cotangent, inverse, weights, filters, window, rows_total, rim):
    outs, padded, d = cotangent.shape
    shares, columns, _ = inverse.shape
    taps, share, _ = weights.shape
    dma = pltpu.SemaphoreType.DMA
    return pl.pallas_call(
        lambda *refs: back_kernel(window, *refs),
        grid=(outs,),
        in_specs=[
            whole(cotangent.shape),
            whole(inverse.shape),
            whole(weights.shape),
            pl.BlockSpec((1,) + filters.shape[1:], lambda i: (i, 0, 0, 0)),
        ],
        out_specs=[
            pl.BlockSpec((1, columns, d), lambda i: (i, 0, 0)),
            whole((rows_total, share, columns)),
            whole((rim, share, columns)),
            whole((rim, share, columns)),
        ],
        out_shape=[
            jax.ShapeDtypeStruct((outs, columns, d), BF16),
            jax.ShapeDtypeStruct((rows_total, share, columns), F32),
            jax.ShapeDtypeStruct((rim, share, columns), BF16),
            jax.ShapeDtypeStruct((rim, share, columns), BF16),
        ],
        scratch_shapes=[
            pltpu.VMEM((taps, share, columns), F32),
            pltpu.VMEM((shares, outs, padded, d), BF16),
            pltpu.VMEM((2, rim, share, columns), BF16),
            pltpu.VMEM((2, rim, share, columns), BF16),
            dma((shares, outs)),
            dma((shares, outs)),
            dma((2,)),
            dma((2,)),
        ],
        compiler_params=remote_params(1),
        cost_estimate=cost(2e10, 1e7),
    )(cotangent, inverse, weights, filters)


def field_grad_kernel(sg_ref, low_ref, high_ref, table_ref, out_ref):
    i = pl.program_id(0)
    last = pl.num_programs(0) - 1
    rows, share, columns = sg_ref.shape
    low = jnp.where(i == 0, low_ref[...].astype(F32), 0.0)
    high = jnp.where(i == last, high_ref[...].astype(F32), 0.0)
    value = (sg_ref[...] + low + high).astype(BF16).reshape(rows * share, columns)
    for s in range(table_ref.shape[0]):
        piece = jnp.dot(value, table_ref[s], preferred_element_type=F32)
        out_ref[s] = piece.astype(BF16).reshape(rows, share, piece.shape[1])


def field_gradient(sg, low, high, table):
    rim, share, columns = low.shape
    rows = sg.shape[0] - 2 * rim
    shares, _, part = table.shape
    return pl.pallas_call(
        field_grad_kernel,
        grid=(rows // rim,),
        in_specs=[
            pl.BlockSpec((rim, share, columns), lambda i: (i + 1, 0, 0)),
            whole(low.shape),
            whole(high.shape),
            whole(table.shape),
        ],
        out_specs=pl.BlockSpec((shares, rim, share, part), lambda i: (0, i, 0, 0)),
        out_shape=jax.ShapeDtypeStruct((shares, rows, share, part), BF16),
        compiler_params=params(),
        cost_estimate=cost(5e9, 6e6),
    )(sg, low, high, table)


def mix_kernel(window, x_ref, table_ref, mk_ref, gs_ref, wt_ref, inv_ref,
               conv_ref, wg_ref, ext_ref, mixed_ref, total_ref,
               conv_send, conv_recv, piece_send, piece_recv, sums, rim_send, rim_recv,
               rim_out_sem, rim_in_sem, conv_out_sem, conv_in_sem, piece_out_sem, piece_in_sem, sum_out_sem, sum_in_sem):
    o = pl.program_id(0)
    _, rows, share, length = x_ref.shape
    columns = table_ref.shape[2]
    rim = rim_send.shape[1]
    taps = mixed_ref.shape[0]
    wide = columns // 2
    block = min(ROWS, share)
    shares, outs = conv_send.shape[:2]
    count, piece = piece_send.shape[:2]
    part = conv_ref.shape[1]
    me = lax.axis_index("azimuth")
    bands = lax.axis_size("polar")
    rank = lax.axis_index("ens") * bands + lax.axis_index("polar")

    def across(step):
        other = lax.rem(me + step, shares)
        return other, {"azimuth": other}

    def along(step):
        other = lax.rem(rank + step, count)
        return other, {"ens": lax.div(other, bands), "polar": lax.rem(other, bands)}

    def conv_copy(row, step):
        other, device = across(step)
        return pltpu.make_async_remote_copy(
            src_ref=conv_send.at[other, row],
            dst_ref=conv_recv.at[me, row],
            send_sem=conv_out_sem.at[step, row],
            recv_sem=conv_in_sem.at[me, row],
            device_id=device,
            device_id_type=pl.DeviceIdType.MESH,
        )

    def conv_arrival(row, step):
        other, device = across(step)
        return pltpu.make_async_remote_copy(
            src_ref=conv_send.at[other, row],
            dst_ref=conv_recv.at[other, row],
            send_sem=conv_out_sem.at[step, row],
            recv_sem=conv_in_sem.at[other, row],
            device_id=device,
            device_id_type=pl.DeviceIdType.MESH,
        )

    def piece_copy(step, landing):
        other, device = along(step)
        at = rank if landing is None else other
        return pltpu.make_async_remote_copy(
            src_ref=piece_send.at[other],
            dst_ref=piece_recv.at[at],
            send_sem=piece_out_sem.at[step],
            recv_sem=piece_in_sem.at[at],
            device_id=device,
            device_id_type=pl.DeviceIdType.MESH,
        )

    def sum_copy(step, landing):
        other, device = along(step)
        at = rank if landing is None else other
        return pltpu.make_async_remote_copy(
            src_ref=sums.at[at],
            dst_ref=sums.at[at],
            send_sem=sum_out_sem.at[step],
            recv_sem=sum_in_sem.at[at],
            device_id=device,
            device_id_type=pl.DeviceIdType.MESH,
        )

    @pl.when(o == 0)
    def _():
        barrier = pltpu.get_barrier_semaphore()
        for step in range(1, shares):
            pl.semaphore_signal(
                barrier, inc=1, device_id=across(step)[1], device_id_type=pl.DeviceIdType.MESH
            )
        for step in range(1, count):
            pl.semaphore_signal(
                barrier, inc=1, device_id=along(step)[1], device_id_type=pl.DeviceIdType.MESH
            )
        pl.semaphore_wait(barrier, shares + count - 2)

        def spectra(first):
            value = None
            for s in range(shares):
                field = x_ref[s, first : first + rim].reshape(rim * share, length)
                term = jnp.dot(field, table_ref[s], preferred_element_type=F32)
                value = term if value is None else value + term
            value = value.reshape(rim, share, columns)
            ext_ref[rim + first : 2 * rim + first] = value
            return value

        copies = rim_copies(rim_send, rim_recv, rim_out_sem, rim_in_sem)
        rim_send[0] = spectra(0).astype(BF16)
        copies[0].start()
        rim_send[1] = spectra(rows - rim).astype(BF16)
        copies[1].start()
        for first in range(rim, rows - rim, rim):
            spectra(first)
        for copy in copies:
            copy.wait_recv()
        low, high = rim_values(rim_recv)
        ext_ref[0:rim] = low
        ext_ref[rim + rows :] = high
        for copy in copies:
            copy.wait_send()
        total_ref[...] = jnp.zeros_like(total_ref)

    for at in range(0, wide, LANES):
        re = slice(at, at + LANES)
        im = slice(wide + at, wide + at + LANES)

        @pl.loop(0, share // block)
        def _(c):
            here = pl.ds(pl.multiple_of(c * block, block), block)
            xr = [ext_ref[2 * o + j, here, re] for j in range(window)]
            xi = [ext_ref[2 * o + j, here, im] for j in range(window)]
            for k in range(taps):
                mr = mi = None
                for j in range(window):
                    pr = mk_ref[0, k, 2 * j : 2 * j + 1, re]
                    pi = mk_ref[0, k, 2 * j + 1 : 2 * j + 2, re]
                    tr = pr * xr[j] - pi * xi[j]
                    ti = pr * xi[j] + pi * xr[j]
                    mr = tr if j == 0 else mr + tr
                    mi = ti if j == 0 else mi + ti
                mixed_ref[k, here, re] = mr.astype(BF16)
                mixed_ref[k, here, im] = mi.astype(BF16)

    mixed = mixed_ref[...].reshape(taps * share, columns)
    total_ref[0 : taps * share] += jnp.dot(mixed, gs_ref[0], preferred_element_type=F32)

    @pl.when(o == outs - 1)
    def _():
        for p in range(count):
            piece_send[p] = total_ref[p * piece : (p + 1) * piece].astype(BF16)
        for step in range(1, count):
            piece_copy(step, None).start()
        piece_recv[rank] = piece_send[rank]

    spec = jnp.dot(wt_ref[...], mixed, preferred_element_type=F32).astype(BF16)
    for step in list(range(1, shares)) + [0]:
        other = across(step)[0]
        term = lax.dot_general(inv_ref[other], spec, NT, preferred_element_type=F32).astype(BF16)
        if step == 0:
            conv_recv[me, o] = term
        else:
            conv_send[other, o] = term
            conv_copy(o, step).start()

    @pl.when(o == outs - 1)
    def _():
        for step in range(1, count):
            piece_copy(step, True).wait_recv()
        whole_sum = piece_recv[0].astype(F32)
        for p in range(1, count):
            whole_sum += piece_recv[p].astype(F32)
        sums[rank] = whole_sum.astype(BF16)
        for step in range(1, count):
            sum_copy(step, None).start()
        for row in range(outs):
            for step in range(1, shares):
                conv_arrival(row, step).wait_recv()
        for row in range(outs):
            result = conv_recv[0, row].astype(F32)
            for s in range(1, shares):
                result += conv_recv[s, row].astype(F32)
            conv_ref[row] = result.astype(BF16)[:part]
        for step in range(1, count):
            sum_copy(step, True).wait_recv()
        wg_ref[...] = sums[...].astype(F32).reshape(count * piece, -1)[: taps * share]
        for row in range(outs):
            for step in range(1, shares):
                conv_copy(row, step).wait_send()
        for step in range(1, count):
            piece_copy(step, None).wait_send()
            sum_copy(step, None).wait_send()


def mix(x, table, filters, gs, weights_t, inverse_t, window, part):
    _, rows, share, _ = x.shape
    columns = table.shape[2]
    rim = window // 2
    outs, taps = filters.shape[:2]
    d = gs.shape[2]
    shares, padded, _ = inverse_t.shape
    count = lax.axis_size("ens") * lax.axis_size("polar")
    piece = -(-taps * share // (count * ROWS)) * ROWS
    dma = pltpu.SemaphoreType.DMA
    return pl.pallas_call(
        lambda *refs: mix_kernel(window, *refs),
        grid=(outs,),
        in_specs=[
            whole(x.shape),
            whole(table.shape),
            pl.BlockSpec((1,) + filters.shape[1:], lambda i: (i, 0, 0, 0)),
            pl.BlockSpec((1, columns, d), lambda i: (i, 0, 0)),
            whole(weights_t.shape),
            whole(inverse_t.shape),
        ],
        out_specs=[whole((outs, part, d)), whole((taps * share, d))],
        out_shape=[
            jax.ShapeDtypeStruct((outs, part, d), BF16),
            jax.ShapeDtypeStruct((taps * share, d), F32),
        ],
        scratch_shapes=[
            pltpu.VMEM((rows + 2 * rim, share, columns), F32),
            pltpu.VMEM((taps, share, columns), BF16),
            pltpu.VMEM((count * piece, d), F32),
            pltpu.VMEM((shares, outs, padded, d), BF16),
            pltpu.VMEM((shares, outs, padded, d), BF16),
            pltpu.VMEM((count, piece, d), BF16),
            pltpu.VMEM((count, piece, d), BF16),
            pltpu.VMEM((count, piece, d), BF16),
            pltpu.VMEM((2, rim, share, columns), BF16),
            pltpu.VMEM((2, rim, share, columns), BF16),
            dma((2,)),
            dma((2,)),
            dma((shares, outs)),
            dma((shares, outs)),
            dma((count,)),
            dma((count,)),
            dma((count,)),
            dma((count,)),
        ],
        compiler_params=remote_params(0),
        cost_estimate=cost(2e10, 1e7),
    )(x, table, filters, gs, weights_t, inverse_t)


def local(fields, basis_spectra, support, weights, out_grad):
    shares = lax.axis_size("azimuth")
    window = basis_spectra.shape[2]
    margin = window // 2
    _, rows, part, channels = fields.shape
    share = channels // shares
    taps, _, d = weights.shape
    forward, forward_t, inverse, inverse_t = make_tables(
        part * shares, out_grad.shape[2] * shares, shares
    )
    cotangent = jnp.pad(out_grad[0], ((0, 0), (0, -out_grad.shape[2] % ROWS), (0, 0)))
    pieces = fields[0].reshape(rows, part, shares, share).transpose(2, 0, 3, 1)
    spread = lax.all_to_all(pieces, "azimuth", 0, 0)
    filters = filter_rows(basis_spectra, support)
    own = lax.dynamic_slice_in_dim(weights, lax.axis_index("azimuth") * share, share, 1)
    own_t = own.reshape(taps * share, d).T

    gs, sg, low, high = backward_spectra(
        cotangent, jnp.asarray(inverse), own, filters, window, rows + 2 * margin, margin
    )
    grad_pieces = field_gradient(sg, low, high, jnp.asarray(forward_t))
    grad_back = lax.all_to_all(grad_pieces, "azimuth", 0, 0)

    spread, _ = lax.optimization_barrier((spread, grad_pieces))
    conv_out, weight_grad = mix(
        spread,
        jnp.asarray(forward),
        filters,
        gs,
        own_t,
        jnp.asarray(inverse_t),
        window,
        out_grad.shape[2],
    )
    weight_grad = weight_grad.reshape(taps, share, d)
    field_grad = grad_back.transpose(1, 3, 0, 2).reshape(rows, part, channels)
    return (conv_out[None], field_grad[None], weight_grad)


def solution(mesh):
    placed = (
        P("ens", "polar", "azimuth", None),
        P(None, "polar", None, None),
        P("polar", None),
        P(),
        P("ens", "polar", "azimuth", None),
    )
    return jax.shard_map(
        local,
        mesh=mesh,
        in_specs=placed,
        out_specs=(
            P("ens", "polar", "azimuth", None),
            P("ens", "polar", "azimuth", None),
            P(None, "azimuth", None),
        ),
        check_vma=False,
    )
```

```python
import math

import jax
import jax.numpy as jnp
import ml_dtypes
import numpy as np
from jax import lax
from jax.experimental import pallas as pl
from jax.experimental.pallas import tpu as pltpu
from jax.sharding import PartitionSpec as P

LANES = 128
ROWS = 16
F32 = jnp.float32
BF16 = jnp.bfloat16
NT = (((1,), (1,)), ((), ()))


def padded_modes(modes):
    return -(-modes // LANES) * LANES


def make_tables(width_in, width_out, shares):
    modes = width_out // 2
    wide = padded_modes(modes)
    frequency = np.arange(modes)
    phases = np.arange(width_in)[:, None] * frequency[None, :] % width_in
    angles = (phases.astype(np.float32) * np.float32(2.0 * math.pi / width_in)).astype(np.float64)
    forward = np.zeros((width_in, 2, wide), np.float32)
    forward[:, 0, :modes] = np.cos(angles)
    forward[:, 1, :modes] = -np.sin(angles)
    phases = frequency[:, None] * np.arange(width_out)[None, :] % width_out
    angles = (phases.astype(np.float32) * np.float32(2.0 * math.pi / width_out)).astype(np.float64)
    factors = (np.where(frequency == 0, 1.0, 2.0) / width_in)[:, None]
    inverse = np.zeros((2, wide, width_out), np.float32)
    inverse[0, :modes] = factors * np.cos(angles)
    inverse[1, :modes] = -factors * np.sin(angles)
    forward = forward.reshape(shares, width_in // shares, 2 * wide).astype(ml_dtypes.bfloat16)
    inverse = inverse.reshape(2 * wide, shares, width_out // shares).astype(ml_dtypes.bfloat16)
    return (
        forward,
        np.ascontiguousarray(forward.transpose(0, 2, 1)),
        np.pad(inverse.transpose(1, 0, 2), ((0, 0), (0, 0), (0, -inverse.shape[2] % ROWS))),
        np.pad(inverse.transpose(1, 2, 0), ((0, 0), (0, -inverse.shape[2] % ROWS), (0, 0))),
    )


def filter_rows(basis, support):
    k, outs, window, columns = basis.shape
    modes = columns // 2
    at = jnp.arange(window, dtype=jnp.int32)
    inside = (at[None, :] >= support[:, 0:1]) & (at[None, :] <= support[:, 1:2])
    masked = jnp.where(inside[None, :, :, None], basis, jnp.zeros_like(basis)).astype(F32)
    masked = masked.reshape(k, outs, 2 * window, modes).transpose(1, 0, 2, 3)
    extra = -(2 * window) % 8
    return jnp.pad(masked, ((0, 0), (0, 0), (0, extra), (0, padded_modes(modes) - modes)))


def whole(shape):
    return pl.BlockSpec(shape, lambda i: (0,) * len(shape))


def remote_params(identity):
    return pltpu.CompilerParams(
        dimension_semantics=("arbitrary",),
        vmem_limit_bytes=30 * 1024 * 1024,
        collective_id=identity,
        has_side_effects=True,
    )


def cost(flops, moved):
    return pl.CostEstimate(flops=int(flops), bytes_accessed=int(moved), transcendentals=0)


def rim_copies(send, recv, out_sem, in_sem):
    bands = lax.axis_size("polar")
    band = lax.axis_index("polar")
    return [
        pltpu.make_async_remote_copy(
            src_ref=send.at[side],
            dst_ref=recv.at[1 - side],
            send_sem=out_sem.at[side],
            recv_sem=in_sem.at[1 - side],
            device_id={"polar": lax.rem(band + step, bands)},
            device_id_type=pl.DeviceIdType.MESH,
        )
        for side, step in ((0, bands - 1), (1, 1))
    ]


def rim_values(recv):
    band = lax.axis_index("polar")
    low = jnp.where(band > 0, recv[0].astype(F32), 0.0)
    high = jnp.where(band < lax.axis_size("polar") - 1, recv[1].astype(F32), 0.0)
    return low, high


def back_kernel(window, og_ref, x_ref, inv_ref, w_ref, mk_ref, table_ref,
                gs_ref, spread_ref, out_ref,
                sg_ref, mg_ref, og_all, x_all, rim_send, rim_recv,
                x_out_sem, x_in_sem, og_out_sem, og_in_sem, rim_out_sem, rim_in_sem):
    o = pl.program_id(0)
    shares, outs = og_all.shape[:2]
    taps, share, columns = mg_ref.shape
    rim = rim_send.shape[1]
    me = lax.axis_index("azimuth")
    bands = lax.axis_size("polar")

    def og_copy(row, step, arriving):
        other = lax.rem(me + step, shares)
        at = other if arriving else me
        return pltpu.make_async_remote_copy(
            src_ref=og_ref.at[row],
            dst_ref=og_all.at[at, row],
            send_sem=og_out_sem.at[step, row],
            recv_sem=og_in_sem.at[at, row],
            device_id={"azimuth": other},
            device_id_type=pl.DeviceIdType.MESH,
        )

    def x_copy(step, arriving):
        other = lax.rem(me + step, shares)
        at = other if arriving else me
        return pltpu.make_async_remote_copy(
            src_ref=x_ref.at[other],
            dst_ref=x_all.at[at],
            send_sem=x_out_sem.at[step],
            recv_sem=x_in_sem.at[at],
            device_id={"azimuth": other},
            device_id_type=pl.DeviceIdType.MESH,
        )

    @pl.when(o == 0)
    def _():
        barrier = pltpu.get_barrier_semaphore()
        for step in range(1, shares):
            pl.semaphore_signal(
                barrier,
                inc=1,
                device_id={"azimuth": lax.rem(me + step, shares)},
                device_id_type=pl.DeviceIdType.MESH,
            )
        for step in (1, bands - 1):
            pl.semaphore_signal(
                barrier,
                inc=1,
                device_id={"polar": lax.rem(lax.axis_index("polar") + step, bands)},
                device_id_type=pl.DeviceIdType.MESH,
            )
        pl.semaphore_wait(barrier, shares + 1)
        for row in range(outs):
            for step in range(1, shares):
                og_copy(row, step, False).start()
        for step in range(1, shares):
            x_copy(step, False).start()
        spread_ref[me] = x_ref[me]

    wide = columns // 2
    block = min(ROWS, share)

    @pl.when(o == 0)
    def _():
        sg_ref[...] = jnp.zeros_like(sg_ref)

    total = jnp.dot(inv_ref[me], og_ref[o], preferred_element_type=F32)
    for step in range(1, shares):
        other = lax.rem(me + step, shares)
        og_copy(o, step, True).wait_recv()
        total += jnp.dot(inv_ref[other], og_all[other, o], preferred_element_type=F32)
    gs = total.astype(BF16)
    gs_ref[0] = gs
    for k in range(taps):
        mg_ref[k] = lax.dot_general(w_ref[k], gs, NT, preferred_element_type=F32)

    for at in range(0, wide, LANES):
        re = slice(at, at + LANES)
        im = slice(wide + at, wide + at + LANES)

        @pl.loop(0, share // block)
        def _(c):
            rows = pl.ds(pl.multiple_of(c * block, block), block)
            acc = [[None, None] for _ in range(window)]
            for k in range(taps):
                gr = mg_ref[k, rows, re]
                gi = mg_ref[k, rows, im]
                for j in range(window):
                    pr = mk_ref[0, k, 2 * j : 2 * j + 1, re]
                    pi = mk_ref[0, k, 2 * j + 1 : 2 * j + 2, re]
                    br = pr * gr + pi * gi
                    bi = pr * gi - pi * gr
                    acc[j][0] = br if k == 0 else acc[j][0] + br
                    acc[j][1] = bi if k == 0 else acc[j][1] + bi
            for j in range(window):
                sg_ref[2 * o + j, rows, re] += acc[j][0]
                sg_ref[2 * o + j, rows, im] += acc[j][1]


    @pl.when(o == outs - 1)
    def _():
        copies = rim_copies(rim_send, rim_recv, rim_out_sem, rim_in_sem)
        rim_send[0] = sg_ref[0:rim].astype(BF16)
        rim_send[1] = sg_ref[sg_ref.shape[0] - rim :].astype(BF16)
        for copy in copies:
            copy.start()
        for copy in copies:
            copy.wait_recv()
        low, high = rim_values(rim_recv)
        total_rows = sg_ref.shape[0]
        sg_ref[rim : 2 * rim] += low
        sg_ref[total_rows - 2 * rim : total_rows - rim] += high
        for first in range(0, total_rows - 2 * rim, rim):
            value = sg_ref[rim + first : 2 * rim + first].astype(BF16)
            value = value.reshape(rim * share, columns)
            for s in range(shares):
                piece = jnp.dot(value, table_ref[s], preferred_element_type=F32)
                out_ref[s, first : first + rim] = piece.astype(BF16).reshape(rim, share, -1)
        for step in range(1, shares):
            other = lax.rem(me + step, shares)
            x_copy(step, True).wait_recv()
            spread_ref[other] = x_all[other]
            x_copy(step, False).wait_send()
        for copy in copies:
            copy.wait_send()
        for row in range(outs):
            for step in range(1, shares):
                og_copy(row, step, False).wait_send()


def backward(cotangent, pieces, inverse, weights, filters, table, window):
    outs, padded, d = cotangent.shape
    shares, columns, _ = inverse.shape
    taps, share, _ = weights.shape
    rim = window // 2
    rows_total = pieces.shape[1] + 2 * rim
    dma = pltpu.SemaphoreType.DMA
    return pl.pallas_call(
        lambda *refs: back_kernel(window, *refs),
        grid=(outs,),
        in_specs=[
            whole(cotangent.shape),
            whole(pieces.shape),
            whole(inverse.shape),
            whole(weights.shape),
            pl.BlockSpec((1,) + filters.shape[1:], lambda i: (i, 0, 0, 0)),
            whole(table.shape),
        ],
        out_specs=[
            pl.BlockSpec((1, columns, d), lambda i: (i, 0, 0)),
            whole(pieces.shape),
            whole(pieces.shape),
        ],
        out_shape=[
            jax.ShapeDtypeStruct((outs, columns, d), BF16),
            jax.ShapeDtypeStruct(pieces.shape, BF16),
            jax.ShapeDtypeStruct(pieces.shape, BF16),
        ],
        scratch_shapes=[
            pltpu.VMEM((rows_total, share, columns), F32),
            pltpu.VMEM((taps, share, columns), F32),
            pltpu.VMEM((shares, outs, padded, d), BF16),
            pltpu.VMEM(pieces.shape, BF16),
            pltpu.VMEM((2, rim, share, columns), BF16),
            pltpu.VMEM((2, rim, share, columns), BF16),
            dma((shares,)),
            dma((shares,)),
            dma((shares, outs)),
            dma((shares, outs)),
            dma((2,)),
            dma((2,)),
        ],
        compiler_params=remote_params(1),
        cost_estimate=cost(2e10, 1e7),
    )(cotangent, pieces, inverse, weights, filters, table)


def mix_kernel(window, x_ref, table_ref, mk_ref, gs_ref, wt_ref, inv_ref,
               conv_ref, wg_ref, ext_ref, mixed_ref, total_ref,
               conv_send, conv_recv, piece_send, piece_recv, sums, rim_send, rim_recv,
               rim_out_sem, rim_in_sem, conv_out_sem, conv_in_sem, piece_out_sem, piece_in_sem, sum_out_sem, sum_in_sem):
    o = pl.program_id(0)
    _, rows, share, length = x_ref.shape
    columns = table_ref.shape[2]
    rim = rim_send.shape[1]
    taps = mixed_ref.shape[0]
    wide = columns // 2
    block = min(ROWS, share)
    shares, outs = conv_send.shape[:2]
    count, piece = piece_send.shape[:2]
    part = conv_ref.shape[1]
    me = lax.axis_index("azimuth")
    bands = lax.axis_size("polar")
    rank = lax.axis_index("ens") * bands + lax.axis_index("polar")

    def across(step):
        other = lax.rem(me + step, shares)
        return other, {"azimuth": other}

    def along(step):
        other = lax.rem(rank + step, count)
        return other, {"ens": lax.div(other, bands), "polar": lax.rem(other, bands)}

    def conv_copy(row, step):
        other, device = across(step)
        return pltpu.make_async_remote_copy(
            src_ref=conv_send.at[other, row],
            dst_ref=conv_recv.at[me, row],
            send_sem=conv_out_sem.at[step, row],
            recv_sem=conv_in_sem.at[me, row],
            device_id=device,
            device_id_type=pl.DeviceIdType.MESH,
        )

    def conv_arrival(row, step):
        other, device = across(step)
        return pltpu.make_async_remote_copy(
            src_ref=conv_send.at[other, row],
            dst_ref=conv_recv.at[other, row],
            send_sem=conv_out_sem.at[step, row],
            recv_sem=conv_in_sem.at[other, row],
            device_id=device,
            device_id_type=pl.DeviceIdType.MESH,
        )

    def piece_copy(step, landing):
        other, device = along(step)
        at = rank if landing is None else other
        return pltpu.make_async_remote_copy(
            src_ref=piece_send.at[other],
            dst_ref=piece_recv.at[at],
            send_sem=piece_out_sem.at[step],
            recv_sem=piece_in_sem.at[at],
            device_id=device,
            device_id_type=pl.DeviceIdType.MESH,
        )

    def sum_copy(step, landing):
        other, device = along(step)
        at = rank if landing is None else other
        return pltpu.make_async_remote_copy(
            src_ref=sums.at[at],
            dst_ref=sums.at[at],
            send_sem=sum_out_sem.at[step],
            recv_sem=sum_in_sem.at[at],
            device_id=device,
            device_id_type=pl.DeviceIdType.MESH,
        )

    @pl.when(o == 0)
    def _():
        barrier = pltpu.get_barrier_semaphore()
        for step in range(1, shares):
            pl.semaphore_signal(
                barrier, inc=1, device_id=across(step)[1], device_id_type=pl.DeviceIdType.MESH
            )
        for step in range(1, count):
            pl.semaphore_signal(
                barrier, inc=1, device_id=along(step)[1], device_id_type=pl.DeviceIdType.MESH
            )
        pl.semaphore_wait(barrier, shares + count - 2)

        def spectra(first):
            value = None
            for s in range(shares):
                field = x_ref[s, first : first + rim].reshape(rim * share, length)
                term = jnp.dot(field, table_ref[s], preferred_element_type=F32)
                value = term if value is None else value + term
            value = value.reshape(rim, share, columns)
            ext_ref[rim + first : 2 * rim + first] = value
            return value

        copies = rim_copies(rim_send, rim_recv, rim_out_sem, rim_in_sem)
        rim_send[0] = spectra(0).astype(BF16)
        copies[0].start()
        rim_send[1] = spectra(rows - rim).astype(BF16)
        copies[1].start()
        for first in range(rim, rows - rim, rim):
            spectra(first)
        for copy in copies:
            copy.wait_recv()
        low, high = rim_values(rim_recv)
        ext_ref[0:rim] = low
        ext_ref[rim + rows :] = high
        for copy in copies:
            copy.wait_send()
        total_ref[...] = jnp.zeros_like(total_ref)

    for at in range(0, wide, LANES):
        re = slice(at, at + LANES)
        im = slice(wide + at, wide + at + LANES)

        @pl.loop(0, share // block)
        def _(c):
            here = pl.ds(pl.multiple_of(c * block, block), block)
            xr = [ext_ref[2 * o + j, here, re] for j in range(window)]
            xi = [ext_ref[2 * o + j, here, im] for j in range(window)]
            for k in range(taps):
                mr = mi = None
                for j in range(window):
                    pr = mk_ref[0, k, 2 * j : 2 * j + 1, re]
                    pi = mk_ref[0, k, 2 * j + 1 : 2 * j + 2, re]
                    tr = pr * xr[j] - pi * xi[j]
                    ti = pr * xi[j] + pi * xr[j]
                    mr = tr if j == 0 else mr + tr
                    mi = ti if j == 0 else mi + ti
                mixed_ref[k, here, re] = mr.astype(BF16)
                mixed_ref[k, here, im] = mi.astype(BF16)

    mixed = mixed_ref[...].reshape(taps * share, columns)
    total_ref[0 : taps * share] += jnp.dot(mixed, gs_ref[0], preferred_element_type=F32)

    @pl.when(o == outs - 1)
    def _():
        for p in range(count):
            piece_send[p] = total_ref[p * piece : (p + 1) * piece].astype(BF16)
        for step in range(1, count):
            piece_copy(step, None).start()
        piece_recv[rank] = piece_send[rank]

    spec = jnp.dot(wt_ref[...], mixed, preferred_element_type=F32).astype(BF16)
    for step in list(range(1, shares)) + [0]:
        other = across(step)[0]
        term = lax.dot_general(inv_ref[other], spec, NT, preferred_element_type=F32).astype(BF16)
        if step == 0:
            conv_recv[me, o] = term
        else:
            conv_send[other, o] = term
            conv_copy(o, step).start()

    @pl.when(o == outs - 1)
    def _():
        for step in range(1, count):
            piece_copy(step, True).wait_recv()
        whole_sum = piece_recv[0].astype(F32)
        for p in range(1, count):
            whole_sum += piece_recv[p].astype(F32)
        sums[rank] = whole_sum.astype(BF16)
        for step in range(1, count):
            sum_copy(step, None).start()
        for row in range(outs):
            for step in range(1, shares):
                conv_arrival(row, step).wait_recv()
        for row in range(outs):
            result = conv_recv[0, row].astype(F32)
            for s in range(1, shares):
                result += conv_recv[s, row].astype(F32)
            conv_ref[row] = result.astype(BF16)[:part]
        for step in range(1, count):
            sum_copy(step, True).wait_recv()
        wg_ref[...] = sums[...].astype(F32).reshape(count * piece, -1)[: taps * share]
        for row in range(outs):
            for step in range(1, shares):
                conv_copy(row, step).wait_send()
        for step in range(1, count):
            piece_copy(step, None).wait_send()
            sum_copy(step, None).wait_send()


def mix(x, table, filters, gs, weights_t, inverse_t, window, part):
    _, rows, share, _ = x.shape
    columns = table.shape[2]
    rim = window // 2
    outs, taps = filters.shape[:2]
    d = gs.shape[2]
    shares, padded, _ = inverse_t.shape
    count = lax.axis_size("ens") * lax.axis_size("polar")
    piece = -(-taps * share // (count * ROWS)) * ROWS
    dma = pltpu.SemaphoreType.DMA
    return pl.pallas_call(
        lambda *refs: mix_kernel(window, *refs),
        grid=(outs,),
        in_specs=[
            whole(x.shape),
            whole(table.shape),
            pl.BlockSpec((1,) + filters.shape[1:], lambda i: (i, 0, 0, 0)),
            pl.BlockSpec((1, columns, d), lambda i: (i, 0, 0)),
            whole(weights_t.shape),
            whole(inverse_t.shape),
        ],
        out_specs=[whole((outs, part, d)), whole((taps * share, d))],
        out_shape=[
            jax.ShapeDtypeStruct((outs, part, d), BF16),
            jax.ShapeDtypeStruct((taps * share, d), F32),
        ],
        scratch_shapes=[
            pltpu.VMEM((rows + 2 * rim, share, columns), F32),
            pltpu.VMEM((taps, share, columns), BF16),
            pltpu.VMEM((count * piece, d), F32),
            pltpu.VMEM((shares, outs, padded, d), BF16),
            pltpu.VMEM((shares, outs, padded, d), BF16),
            pltpu.VMEM((count, piece, d), BF16),
            pltpu.VMEM((count, piece, d), BF16),
            pltpu.VMEM((count, piece, d), BF16),
            pltpu.VMEM((2, rim, share, columns), BF16),
            pltpu.VMEM((2, rim, share, columns), BF16),
            dma((2,)),
            dma((2,)),
            dma((shares, outs)),
            dma((shares, outs)),
            dma((count,)),
            dma((count,)),
            dma((count,)),
            dma((count,)),
        ],
        compiler_params=remote_params(0),
        cost_estimate=cost(2e10, 1e7),
    )(x, table, filters, gs, weights_t, inverse_t)


def local(fields, basis_spectra, support, weights, out_grad):
    shares = lax.axis_size("azimuth")
    window = basis_spectra.shape[2]
    _, rows, part, channels = fields.shape
    share = channels // shares
    taps, _, d = weights.shape
    forward, forward_t, inverse, inverse_t = make_tables(
        part * shares, out_grad.shape[2] * shares, shares
    )
    cotangent = jnp.pad(out_grad[0], ((0, 0), (0, -out_grad.shape[2] % ROWS), (0, 0)))
    pieces = fields[0].reshape(rows, part, shares, share).transpose(2, 0, 3, 1)
    filters = filter_rows(basis_spectra, support)
    own = lax.dynamic_slice_in_dim(weights, lax.axis_index("azimuth") * share, share, 1)
    own_t = own.reshape(taps * share, d).T

    gs, spread, grad_pieces = backward(
        cotangent, pieces, jnp.asarray(inverse), own, filters, jnp.asarray(forward_t), window
    )
    grad_back = lax.all_to_all(grad_pieces, "azimuth", 0, 0)

    conv_out, weight_grad = mix(
        spread,
        jnp.asarray(forward),
        filters,
        gs,
        own_t,
        jnp.asarray(inverse_t),
        window,
        out_grad.shape[2],
    )
    weight_grad = weight_grad.reshape(taps, share, d)
    field_grad = grad_back.transpose(1, 3, 0, 2).reshape(rows, part, channels)
    return (conv_out[None], field_grad[None], weight_grad)


def solution(mesh):
    placed = (
        P("ens", "polar", "azimuth", None),
        P(None, "polar", None, None),
        P("polar", None),
        P(),
        P("ens", "polar", "azimuth", None),
    )
    return jax.shard_map(
        local,
        mesh=mesh,
        in_specs=placed,
        out_specs=(
            P("ens", "polar", "azimuth", None),
            P("ens", "polar", "azimuth", None),
            P(None, "azimuth", None),
        ),
        check_vma=False,
    )
```

```python
import math

import jax
import jax.numpy as jnp
import ml_dtypes
import numpy as np
from jax import lax
from jax.experimental import pallas as pl
from jax.experimental.pallas import tpu as pltpu
from jax.sharding import PartitionSpec as P

LANES = 128
ROWS = 16
F32 = jnp.float32
BF16 = jnp.bfloat16
NT = (((1,), (1,)), ((), ()))


def padded_modes(modes):
    return -(-modes // LANES) * LANES


def make_tables(width_in, width_out, shares):
    modes = width_out // 2
    wide = padded_modes(modes)
    frequency = np.arange(modes)
    phases = np.arange(width_in)[:, None] * frequency[None, :] % width_in
    angles = (phases.astype(np.float32) * np.float32(2.0 * math.pi / width_in)).astype(np.float64)
    forward = np.zeros((width_in, 2, wide), np.float32)
    forward[:, 0, :modes] = np.cos(angles)
    forward[:, 1, :modes] = -np.sin(angles)
    phases = frequency[:, None] * np.arange(width_out)[None, :] % width_out
    angles = (phases.astype(np.float32) * np.float32(2.0 * math.pi / width_out)).astype(np.float64)
    factors = (np.where(frequency == 0, 1.0, 2.0) / width_in)[:, None]
    inverse = np.zeros((2, wide, width_out), np.float32)
    inverse[0, :modes] = factors * np.cos(angles)
    inverse[1, :modes] = -factors * np.sin(angles)
    forward = forward.reshape(shares, width_in // shares, 2 * wide).astype(ml_dtypes.bfloat16)
    inverse = inverse.reshape(2 * wide, shares, width_out // shares).astype(ml_dtypes.bfloat16)
    return (
        forward,
        np.ascontiguousarray(forward.transpose(0, 2, 1)),
        np.pad(inverse.transpose(1, 0, 2), ((0, 0), (0, 0), (0, -inverse.shape[2] % ROWS))),
        np.pad(inverse.transpose(1, 2, 0), ((0, 0), (0, -inverse.shape[2] % ROWS), (0, 0))),
    )


def filter_rows(basis, support):
    k, outs, window, columns = basis.shape
    modes = columns // 2
    at = jnp.arange(window, dtype=jnp.int32)
    inside = (at[None, :] >= support[:, 0:1]) & (at[None, :] <= support[:, 1:2])
    masked = jnp.where(inside[None, :, :, None], basis, jnp.zeros_like(basis)).astype(F32)
    masked = masked.reshape(k, outs, 2 * window, modes).transpose(1, 0, 2, 3)
    extra = -(2 * window) % 8
    return jnp.pad(masked, ((0, 0), (0, 0), (0, extra), (0, padded_modes(modes) - modes)))


def whole(shape):
    return pl.BlockSpec(shape, lambda i: (0,) * len(shape))


def remote_params(identity):
    return pltpu.CompilerParams(
        dimension_semantics=("arbitrary",),
        vmem_limit_bytes=30 * 1024 * 1024,
        collective_id=identity,
        has_side_effects=True,
    )


def cost(flops, moved):
    return pl.CostEstimate(flops=int(flops), bytes_accessed=int(moved), transcendentals=0)


def rim_copies(send, recv, out_sem, in_sem):
    bands = lax.axis_size("polar")
    band = lax.axis_index("polar")
    return [
        pltpu.make_async_remote_copy(
            src_ref=send.at[side],
            dst_ref=recv.at[1 - side],
            send_sem=out_sem.at[side],
            recv_sem=in_sem.at[1 - side],
            device_id={"polar": lax.rem(band + step, bands)},
            device_id_type=pl.DeviceIdType.MESH,
        )
        for side, step in ((0, bands - 1), (1, 1))
    ]


def rim_values(recv):
    band = lax.axis_index("polar")
    low = jnp.where(band > 0, recv[0].astype(F32), 0.0)
    high = jnp.where(band < lax.axis_size("polar") - 1, recv[1].astype(F32), 0.0)
    return low, high


def back_kernel(window, og_ref, x_ref, inv_ref, w_ref, mk_ref, table_ref,
                gs_ref, spread_ref, out_ref,
                sg_ref, mg_ref, og_all, x_all, rim_send, rim_recv,
                x_out_sem, x_in_sem, og_out_sem, og_in_sem, rim_out_sem, rim_in_sem):
    o = pl.program_id(0)
    shares, outs = og_all.shape[:2]
    taps, share, columns = mg_ref.shape
    rim = rim_send.shape[1]
    me = lax.axis_index("azimuth")
    bands = lax.axis_size("polar")

    def og_copy(row, step, arriving):
        other = lax.rem(me + step, shares)
        at = other if arriving else me
        return pltpu.make_async_remote_copy(
            src_ref=og_ref.at[row],
            dst_ref=og_all.at[at, row],
            send_sem=og_out_sem.at[step, row],
            recv_sem=og_in_sem.at[at, row],
            device_id={"azimuth": other},
            device_id_type=pl.DeviceIdType.MESH,
        )

    def x_copy(step, arriving):
        other = lax.rem(me + step, shares)
        at = other if arriving else me
        return pltpu.make_async_remote_copy(
            src_ref=x_ref.at[other],
            dst_ref=x_all.at[at],
            send_sem=x_out_sem.at[step],
            recv_sem=x_in_sem.at[at],
            device_id={"azimuth": other},
            device_id_type=pl.DeviceIdType.MESH,
        )

    @pl.when(o == 0)
    def _():
        barrier = pltpu.get_barrier_semaphore()
        for step in range(1, shares):
            pl.semaphore_signal(
                barrier,
                inc=1,
                device_id={"azimuth": lax.rem(me + step, shares)},
                device_id_type=pl.DeviceIdType.MESH,
            )
        for step in (1, bands - 1):
            pl.semaphore_signal(
                barrier,
                inc=1,
                device_id={"polar": lax.rem(lax.axis_index("polar") + step, bands)},
                device_id_type=pl.DeviceIdType.MESH,
            )
        pl.semaphore_wait(barrier, shares + 1)
        for row in range(outs):
            for step in range(1, shares):
                og_copy(row, step, False).start()
        for step in range(1, shares):
            x_copy(step, False).start()
        spread_ref[me] = x_ref[me]

    wide = columns // 2
    block = min(ROWS, share)

    @pl.when(o == 0)
    def _():
        sg_ref[...] = jnp.zeros_like(sg_ref)

    total = jnp.dot(inv_ref[me], og_ref[o], preferred_element_type=F32)
    for step in range(1, shares):
        other = lax.rem(me + step, shares)
        og_copy(o, step, True).wait_recv()
        total += jnp.dot(inv_ref[other], og_all[other, o], preferred_element_type=F32)
    gs = total.astype(BF16)
    gs_ref[0] = gs
    for k in range(taps):
        mg_ref[k] = lax.dot_general(w_ref[k], gs, NT, preferred_element_type=F32)

    for at in range(0, wide, LANES):
        re = slice(at, at + LANES)
        im = slice(wide + at, wide + at + LANES)

        @pl.loop(0, share // block)
        def _(c):
            rows = pl.ds(pl.multiple_of(c * block, block), block)
            acc = [[None, None] for _ in range(window)]
            for k in range(taps):
                gr = mg_ref[k, rows, re]
                gi = mg_ref[k, rows, im]
                for j in range(window):
                    pr = mk_ref[0, k, 2 * j : 2 * j + 1, re]
                    pi = mk_ref[0, k, 2 * j + 1 : 2 * j + 2, re]
                    br = pr * gr + pi * gi
                    bi = pr * gi - pi * gr
                    acc[j][0] = br if k == 0 else acc[j][0] + br
                    acc[j][1] = bi if k == 0 else acc[j][1] + bi
            for j in range(window):
                sg_ref[2 * o + j, rows, re] += acc[j][0]
                sg_ref[2 * o + j, rows, im] += acc[j][1]


    @pl.when(o == outs - 1)
    def _():
        copies = rim_copies(rim_send, rim_recv, rim_out_sem, rim_in_sem)
        rim_send[0] = sg_ref[0:rim].astype(BF16)
        rim_send[1] = sg_ref[sg_ref.shape[0] - rim :].astype(BF16)
        for copy in copies:
            copy.start()
        for copy in copies:
            copy.wait_recv()
        low, high = rim_values(rim_recv)
        total_rows = sg_ref.shape[0]
        sg_ref[rim : 2 * rim] += low
        sg_ref[total_rows - 2 * rim : total_rows - rim] += high
        for first in range(0, total_rows - 2 * rim, rim):
            value = sg_ref[rim + first : 2 * rim + first].astype(BF16)
            value = value.reshape(rim * share, columns)
            for s in range(shares):
                piece = jnp.dot(value, table_ref[s], preferred_element_type=F32)
                out_ref[s, first : first + rim] = piece.astype(BF16).reshape(rim, share, -1)
        for step in range(1, shares):
            other = lax.rem(me + step, shares)
            x_copy(step, True).wait_recv()
            spread_ref[other] = x_all[other]
            x_copy(step, False).wait_send()
        for copy in copies:
            copy.wait_send()
        for row in range(outs):
            for step in range(1, shares):
                og_copy(row, step, False).wait_send()


def backward(cotangent, pieces, inverse, weights, filters, table, window):
    outs, padded, d = cotangent.shape
    shares, columns, _ = inverse.shape
    taps, share, _ = weights.shape
    rim = window // 2
    rows_total = pieces.shape[1] + 2 * rim
    dma = pltpu.SemaphoreType.DMA
    return pl.pallas_call(
        lambda *refs: back_kernel(window, *refs),
        grid=(outs,),
        in_specs=[
            whole(cotangent.shape),
            whole(pieces.shape),
            whole(inverse.shape),
            whole(weights.shape),
            pl.BlockSpec((1,) + filters.shape[1:], lambda i: (i, 0, 0, 0)),
            whole(table.shape),
        ],
        out_specs=[
            pl.BlockSpec((1, columns, d), lambda i: (i, 0, 0)),
            whole(pieces.shape),
            whole(pieces.shape),
        ],
        out_shape=[
            jax.ShapeDtypeStruct((outs, columns, d), BF16),
            jax.ShapeDtypeStruct(pieces.shape, BF16),
            jax.ShapeDtypeStruct(pieces.shape, BF16),
        ],
        scratch_shapes=[
            pltpu.VMEM((rows_total, share, columns), F32),
            pltpu.VMEM((taps, share, columns), F32),
            pltpu.VMEM((shares, outs, padded, d), BF16),
            pltpu.VMEM(pieces.shape, BF16),
            pltpu.VMEM((2, rim, share, columns), BF16),
            pltpu.VMEM((2, rim, share, columns), BF16),
            dma((shares,)),
            dma((shares,)),
            dma((shares, outs)),
            dma((shares, outs)),
            dma((2,)),
            dma((2,)),
        ],
        compiler_params=remote_params(1),
        cost_estimate=cost(2e10, 1e7),
    )(cotangent, pieces, inverse, weights, filters, table)


def mix_kernel(window, fg_ref, x_ref, table_ref, mk_ref, gs_ref, wt_ref, inv_ref,
               conv_ref, wg_ref, back_ref, fg_all, fg_out_sem, fg_in_sem, ext_ref, mixed_ref, total_ref,
               conv_send, conv_recv, piece_send, piece_recv, sums, rim_send, rim_recv,
               rim_out_sem, rim_in_sem, conv_out_sem, conv_in_sem, piece_out_sem, piece_in_sem, sum_out_sem, sum_in_sem):
    o = pl.program_id(0)
    _, rows, share, length = x_ref.shape
    columns = table_ref.shape[2]
    rim = rim_send.shape[1]
    taps = mixed_ref.shape[0]
    wide = columns // 2
    block = min(ROWS, share)
    shares, outs = conv_send.shape[:2]
    count, piece = piece_send.shape[:2]
    part = conv_ref.shape[1]
    me = lax.axis_index("azimuth")
    bands = lax.axis_size("polar")
    rank = lax.axis_index("ens") * bands + lax.axis_index("polar")

    def across(step):
        other = lax.rem(me + step, shares)
        return other, {"azimuth": other}

    def along(step):
        other = lax.rem(rank + step, count)
        return other, {"ens": lax.div(other, bands), "polar": lax.rem(other, bands)}

    def fg_copy(step, arriving):
        other, device = across(step)
        at = other if arriving else me
        return pltpu.make_async_remote_copy(
            src_ref=fg_ref.at[other],
            dst_ref=fg_all.at[at],
            send_sem=fg_out_sem.at[step],
            recv_sem=fg_in_sem.at[at],
            device_id=device,
            device_id_type=pl.DeviceIdType.MESH,
        )

    def conv_copy(row, step):
        other, device = across(step)
        return pltpu.make_async_remote_copy(
            src_ref=conv_send.at[other, row],
            dst_ref=conv_recv.at[me, row],
            send_sem=conv_out_sem.at[step, row],
            recv_sem=conv_in_sem.at[me, row],
            device_id=device,
            device_id_type=pl.DeviceIdType.MESH,
        )

    def conv_arrival(row, step):
        other, device = across(step)
        return pltpu.make_async_remote_copy(
            src_ref=conv_send.at[other, row],
            dst_ref=conv_recv.at[other, row],
            send_sem=conv_out_sem.at[step, row],
            recv_sem=conv_in_sem.at[other, row],
            device_id=device,
            device_id_type=pl.DeviceIdType.MESH,
        )

    def piece_copy(step, landing):
        other, device = along(step)
        at = rank if landing is None else other
        return pltpu.make_async_remote_copy(
            src_ref=piece_send.at[other],
            dst_ref=piece_recv.at[at],
            send_sem=piece_out_sem.at[step],
            recv_sem=piece_in_sem.at[at],
            device_id=device,
            device_id_type=pl.DeviceIdType.MESH,
        )

    def sum_copy(step, landing):
        other, device = along(step)
        at = rank if landing is None else other
        return pltpu.make_async_remote_copy(
            src_ref=sums.at[at],
            dst_ref=sums.at[at],
            send_sem=sum_out_sem.at[step],
            recv_sem=sum_in_sem.at[at],
            device_id=device,
            device_id_type=pl.DeviceIdType.MESH,
        )

    @pl.when(o == 0)
    def _():
        barrier = pltpu.get_barrier_semaphore()
        for step in range(1, shares):
            pl.semaphore_signal(
                barrier, inc=1, device_id=across(step)[1], device_id_type=pl.DeviceIdType.MESH
            )
        for step in range(1, count):
            pl.semaphore_signal(
                barrier, inc=1, device_id=along(step)[1], device_id_type=pl.DeviceIdType.MESH
            )
        pl.semaphore_wait(barrier, shares + count - 2)
        for step in range(1, shares):
            fg_copy(step, False).start()
        back_ref[me] = fg_ref[me]

        def spectra(first):
            value = None
            for s in range(shares):
                field = x_ref[s, first : first + rim].reshape(rim * share, length)
                term = jnp.dot(field, table_ref[s], preferred_element_type=F32)
                value = term if value is None else value + term
            value = value.reshape(rim, share, columns)
            ext_ref[rim + first : 2 * rim + first] = value
            return value

        copies = rim_copies(rim_send, rim_recv, rim_out_sem, rim_in_sem)
        rim_send[0] = spectra(0).astype(BF16)
        copies[0].start()
        rim_send[1] = spectra(rows - rim).astype(BF16)
        copies[1].start()
        for first in range(rim, rows - rim, rim):
            spectra(first)
        for copy in copies:
            copy.wait_recv()
        low, high = rim_values(rim_recv)
        ext_ref[0:rim] = low
        ext_ref[rim + rows :] = high
        for copy in copies:
            copy.wait_send()
        total_ref[...] = jnp.zeros_like(total_ref)

    for at in range(0, wide, LANES):
        re = slice(at, at + LANES)
        im = slice(wide + at, wide + at + LANES)

        @pl.loop(0, share // block)
        def _(c):
            here = pl.ds(pl.multiple_of(c * block, block), block)
            xr = [ext_ref[2 * o + j, here, re] for j in range(window)]
            xi = [ext_ref[2 * o + j, here, im] for j in range(window)]
            for k in range(taps):
                mr = mi = None
                for j in range(window):
                    pr = mk_ref[0, k, 2 * j : 2 * j + 1, re]
                    pi = mk_ref[0, k, 2 * j + 1 : 2 * j + 2, re]
                    tr = pr * xr[j] - pi * xi[j]
                    ti = pr * xi[j] + pi * xr[j]
                    mr = tr if j == 0 else mr + tr
                    mi = ti if j == 0 else mi + ti
                mixed_ref[k, here, re] = mr.astype(BF16)
                mixed_ref[k, here, im] = mi.astype(BF16)

    mixed = mixed_ref[...].reshape(taps * share, columns)
    total_ref[0 : taps * share] += jnp.dot(mixed, gs_ref[0], preferred_element_type=F32)

    @pl.when(o == outs - 1)
    def _():
        for p in range(count):
            piece_send[p] = total_ref[p * piece : (p + 1) * piece].astype(BF16)
        for step in range(1, count):
            piece_copy(step, None).start()
        piece_recv[rank] = piece_send[rank]

    spec = jnp.dot(wt_ref[...], mixed, preferred_element_type=F32).astype(BF16)
    for step in list(range(1, shares)) + [0]:
        other = across(step)[0]
        term = lax.dot_general(inv_ref[other], spec, NT, preferred_element_type=F32).astype(BF16)
        if step == 0:
            conv_recv[me, o] = term
        else:
            conv_send[other, o] = term
            conv_copy(o, step).start()

    @pl.when(o == outs - 1)
    def _():
        for step in range(1, count):
            piece_copy(step, True).wait_recv()
        whole_sum = piece_recv[0].astype(F32)
        for p in range(1, count):
            whole_sum += piece_recv[p].astype(F32)
        sums[rank] = whole_sum.astype(BF16)
        for step in range(1, count):
            sum_copy(step, None).start()
        for step in range(1, shares):
            other = across(step)[0]
            fg_copy(step, True).wait_recv()
            back_ref[other] = fg_all[other]
            fg_copy(step, False).wait_send()
        for row in range(outs):
            for step in range(1, shares):
                conv_arrival(row, step).wait_recv()
        for row in range(outs):
            result = conv_recv[0, row].astype(F32)
            for s in range(1, shares):
                result += conv_recv[s, row].astype(F32)
            conv_ref[row] = result.astype(BF16)[:part]
        for step in range(1, count):
            sum_copy(step, True).wait_recv()
        wg_ref[...] = sums[...].astype(F32).reshape(count * piece, -1)[: taps * share]
        for row in range(outs):
            for step in range(1, shares):
                conv_copy(row, step).wait_send()
        for step in range(1, count):
            piece_copy(step, None).wait_send()
            sum_copy(step, None).wait_send()


def mix(pieces, x, table, filters, gs, weights_t, inverse_t, window, part):
    _, rows, share, _ = x.shape
    columns = table.shape[2]
    rim = window // 2
    outs, taps = filters.shape[:2]
    d = gs.shape[2]
    shares, padded, _ = inverse_t.shape
    count = lax.axis_size("ens") * lax.axis_size("polar")
    piece = -(-taps * share // (count * ROWS)) * ROWS
    dma = pltpu.SemaphoreType.DMA
    return pl.pallas_call(
        lambda *refs: mix_kernel(window, *refs),
        grid=(outs,),
        in_specs=[
            whole(pieces.shape),
            whole(x.shape),
            whole(table.shape),
            pl.BlockSpec((1,) + filters.shape[1:], lambda i: (i, 0, 0, 0)),
            pl.BlockSpec((1, columns, d), lambda i: (i, 0, 0)),
            whole(weights_t.shape),
            whole(inverse_t.shape),
        ],
        out_specs=[whole((outs, part, d)), whole((taps * share, d)), whole(pieces.shape)],
        out_shape=[
            jax.ShapeDtypeStruct((outs, part, d), BF16),
            jax.ShapeDtypeStruct((taps * share, d), F32),
            jax.ShapeDtypeStruct(pieces.shape, BF16),
        ],
        scratch_shapes=[
            pltpu.VMEM(pieces.shape, BF16),
            dma((shares,)),
            dma((shares,)),
            pltpu.VMEM((rows + 2 * rim, share, columns), F32),
            pltpu.VMEM((taps, share, columns), BF16),
            pltpu.VMEM((count * piece, d), F32),
            pltpu.VMEM((shares, outs, padded, d), BF16),
            pltpu.VMEM((shares, outs, padded, d), BF16),
            pltpu.VMEM((count, piece, d), BF16),
            pltpu.VMEM((count, piece, d), BF16),
            pltpu.VMEM((count, piece, d), BF16),
            pltpu.VMEM((2, rim, share, columns), BF16),
            pltpu.VMEM((2, rim, share, columns), BF16),
            dma((2,)),
            dma((2,)),
            dma((shares, outs)),
            dma((shares, outs)),
            dma((count,)),
            dma((count,)),
            dma((count,)),
            dma((count,)),
        ],
        compiler_params=remote_params(0),
        cost_estimate=cost(2e10, 1e7),
    )(pieces, x, table, filters, gs, weights_t, inverse_t)


def local(fields, basis_spectra, support, weights, out_grad):
    shares = lax.axis_size("azimuth")
    window = basis_spectra.shape[2]
    _, rows, part, channels = fields.shape
    share = channels // shares
    taps, _, d = weights.shape
    forward, forward_t, inverse, inverse_t = make_tables(
        part * shares, out_grad.shape[2] * shares, shares
    )
    cotangent = jnp.pad(out_grad[0], ((0, 0), (0, -out_grad.shape[2] % ROWS), (0, 0)))
    pieces = fields[0].reshape(rows, part, shares, share).transpose(2, 0, 3, 1)
    filters = filter_rows(basis_spectra, support)
    own = lax.dynamic_slice_in_dim(weights, lax.axis_index("azimuth") * share, share, 1)
    own_t = own.reshape(taps * share, d).T

    gs, spread, grad_pieces = backward(
        cotangent, pieces, jnp.asarray(inverse), own, filters, jnp.asarray(forward_t), window
    )

    conv_out, weight_grad, grad_back = mix(
        grad_pieces,
        spread,
        jnp.asarray(forward),
        filters,
        gs,
        own_t,
        jnp.asarray(inverse_t),
        window,
        out_grad.shape[2],
    )
    weight_grad = weight_grad.reshape(taps, share, d)
    field_grad = grad_back.transpose(1, 3, 0, 2).reshape(rows, part, channels)
    return (conv_out[None], field_grad[None], weight_grad)


def solution(mesh):
    placed = (
        P("ens", "polar", "azimuth", None),
        P(None, "polar", None, None),
        P("polar", None),
        P(),
        P("ens", "polar", "azimuth", None),
    )
    return jax.shard_map(
        local,
        mesh=mesh,
        in_specs=placed,
        out_specs=(
            P("ens", "polar", "azimuth", None),
            P("ens", "polar", "azimuth", None),
            P(None, "azimuth", None),
        ),
        check_vma=False,
    )
```
